512 devices in a mesh: col: 8 (over y_lo, core), dev: 64 (over y_hi, z, x).
Axes of the slice: x: 4, y: 8 (y_hi: 2, y_lo: 4; y = y_hi * 4 + y_lo), z: 8, core: 2. Of those that a mesh axis runs over, the one named last changes fastest.
Arguments:
- factor_a: float32 [1536, 16, 512], P('dev'), may hold values from -1 to 1
- factor_b: float32 [1536, 64, 512], P('dev', 'col'), may hold values from -1 to 1
- factor_occ: float32 [1536, 16, 512], P('dev'), may hold values from -1 to 1
- singles_a: float32 [16, 16], replicated, may hold values from -1.5 to 1.5
- singles_b: float32 [16, 64], P(None, 'col'), may hold values from -1.5 to 1.5
- doubles: bfloat16 [512, 512, 256], P('col', 'dev'), may hold values from -0.023925781 to 0.023925781
- orbital_a: float32 [16], P('col'), may hold values from 0.2 to 3
- orbital_b: float32 [64], P('dev'), may hold values from 0.2 to 3
- orbital_occ: float32 [16], replicated, may hold values from -2 to -0.3
Outputs:
- update: float32 [16, 64, 256], P('col', 'dev')
The draws below stay inside these ranges and needn't reach their ends.
All inputs are finite; a program needn't handle non-finite values.
Results may differ from the reference program's by a relative error of at most 0.0049.
Values may be sent and summed in bfloat16 or wider, within the bound.
A program may use at most 64 MiB of HBM per device.

```python
import jax
import jax.numpy as jnp
from jax import lax

V = 512
NAUX = 1536
O = 16
A = 16
B = 64
PAIRS = 256


def block_scale(own_key, dims, pieces, smallest, top_value):
    level, own = 1.0, jax.random.fold_in(own_key, 6)
    for position, parts in pieces:
        draws = jnp.exp(jax.random.uniform(jax.random.fold_in(own, position), (parts,), jnp.float32, smallest / len(pieces), top_value / len(pieces)))
        level = level * jnp.repeat(draws, dims[position] // parts).reshape([-1 if axis == position else 1 for axis in range(len(dims))])
    return level


def noise(stream_key, shape, scale, bound, pieces=(), held_as=jnp.bfloat16):
    drawn = scale * jax.random.normal(stream_key, shape, jnp.float32)
    if pieces:
        drawn = drawn * block_scale(stream_key, shape, pieces, -0.22, 0.18)
    return jnp.clip(drawn, -bound, bound).astype(held_as)


def setup_inputs(seed: int = 0) -> dict:
    arg_keys = jax.random.split(jax.random.key(seed), 10)
    return {
        "factor_a": noise(arg_keys[0], (NAUX, A, V), 0.16, 1.0, ((0, 64),), jnp.float32),
        "factor_b": noise(arg_keys[1], (NAUX, B, V), 0.16, 1.0, ((0, 64), (1, 8)), jnp.float32),
        "factor_occ": noise(arg_keys[2], (NAUX, O, V), 0.16, 1.0, ((0, 64),), jnp.float32),
        "singles_a": noise(arg_keys[3], (O, A), 0.25, 1.5, (), jnp.float32),
        "singles_b": noise(arg_keys[4], (O, B), 0.25, 1.5, ((1, 8),), jnp.float32),
        "doubles": noise(arg_keys[5], (V, V, PAIRS), 0.004, 0.023925781, ((0, 8), (1, 64))),
        "orbital_a": jnp.clip(0.2 + 2.8 * jax.random.uniform(arg_keys[6], (A,), jnp.float32) ** block_scale(arg_keys[6], (A,), ((0, 8),), -0.2, 0.2), 0.2, 3.0),
        "orbital_b": jnp.clip(0.2 + 2.8 * jax.random.uniform(arg_keys[7], (B,), jnp.float32) ** block_scale(arg_keys[7], (B,), ((0, 64),), -0.2, 0.2), 0.2, 3.0),
        "orbital_occ": jnp.clip(jax.random.uniform(arg_keys[8], (O,), jnp.float32, -2.0, -0.3), -2.0, -0.3),
    }


def reference(factor_a, factor_b, factor_occ, singles_a, singles_b, doubles, orbital_a, orbital_b, orbital_occ):
    highest = lax.Precision.HIGHEST
    dressed_a = (factor_a - jnp.einsum("ka,qkc->qac", singles_a, factor_occ, precision=highest)).astype(jnp.bfloat16)
    dressed_b = (factor_b - jnp.einsum("kb,qkd->qbd", singles_b, factor_occ, precision=highest)).astype(jnp.bfloat16)
    wide_b = dressed_b.astype(jnp.float32)
    amplitude = doubles.astype(jnp.float32)

    def one_row(row_a):
        integral = jnp.einsum("qc,qbd->cbd", row_a.astype(jnp.float32), wide_b, precision=highest)
        integral = lax.optimization_barrier(integral.astype(jnp.bfloat16)).astype(jnp.float32)
        return jnp.einsum("cbd,cdp->bp", integral, amplitude, precision=highest)

    residual = lax.map(one_row, jnp.transpose(dressed_a, (1, 0, 2)))
    pair_energy = (orbital_occ[:, None] + orbital_occ[None, :]).reshape(-1)
    denominator = orbital_a[:, None, None] + orbital_b[None, :, None] - pair_energy[None, None, :]
    return residual / denominator
```

```python
import jax
import jax.numpy as jnp
from jax import lax
from jax.experimental import pallas as pl
from jax.experimental.pallas import tpu as pltpu
from jax.sharding import PartitionSpec as P

MESH = pl.DeviceIdType.MESH
F32 = jnp.float32
BF16 = jnp.bfloat16
HIGHEST = lax.Precision.HIGHEST
NH, NZ, NX, NL, NK = 2, 8, 4, 4, 2


def lanes_of(shape):
    return lax.broadcasted_iota(jnp.int32, shape, len(shape) - 1)


def rows_of(shape):
    return lax.broadcasted_iota(jnp.int32, shape, 0)


def spread(singles, rows):
    pick = (rows_of((rows * 8, rows)) // 8 == lanes_of((rows * 8, rows))).astype(F32)
    across = (rows_of((16, 128)) == lanes_of((16, 128)) % 16).astype(F32)
    first = lax.dot_general(pick, singles, (((1,), (1,)), ((), ())), precision=HIGHEST)
    full = jnp.dot(first, across, precision=HIGHEST)
    same = rows_of((rows * 8, 128)) % 8 == lanes_of((rows * 8, 128)) // 16
    return jnp.where(same, full, 0.0)


def strided(ref, start, size, stride):
    tiles = [ref[t, pl.ds(start, size, stride=stride), :] for t in range(ref.shape[0])]
    return jnp.concatenate(tiles, axis=1)


def put(ref, value):
    for t in range(ref.shape[0]):
        ref[t] = value[:, t * 128 : (t + 1) * 128]


def kernel(
    fa, fb, fo, sa, sb, tau, oa, ob, oo, out,
    fo_v, fb_v, fa_v, tau_v, tf_v,
    b1_send, b1_recv, b2_send, b_all, bt_all,
    a_blk, a_mir, a_all, t_all, integral, acc_p, acc_o,
    c_send, c_recv, x_send, x_recv, s_v, z_send, z_recv, s2_v, y_send, y_recv,
    load_sem, b1_ss, b1_rs, b2_ss, b2_rs, fw_ss, fw_rs, am_ss, am_rs, a_ss, a_rs,
    t_ss, t_rs, c_ss, c_rs, x_ss, x_rs, z_ss, z_rs, y_ss, y_rs,
):
    col = lax.axis_index("col")
    dev = lax.axis_index("dev")
    l, k = col // NK, col % NK
    h, z, x = dev // (NZ * NX), (dev // NX) % NZ, dev % NX

    def col_id(l_, k_):
        return l_ * NK + k_

    def dev_id(h_, z_, x_):
        return (h_ * NZ + z_) * NX + x_

    def at(h_=h, z_=z, x_=x, l_=l, k_=k):
        return (col_id(l_, k_), dev_id(h_, z_, x_))

    def remote(src, dst, ss, rs, target):
        return pltpu.make_async_remote_copy(
            src_ref=src, dst_ref=dst, send_sem=ss, recv_sem=rs, device_id=target, device_id_type=MESH
        )

    def wait_recv(dst, ss, rs):
        remote(dst, dst, ss, rs, at(k_=1 - k)).wait_recv()

    hl, ml = h, NL - 1 - l
    own_lanes = pl.ds(pl.multiple_of(l * 128, 128), 128)
    mir_lanes = pl.ds(pl.multiple_of(ml * 128, 128), 128)
    loads = [
        pltpu.make_async_copy(fo, fo_v, load_sem.at[0]),
        pltpu.make_async_copy(fb.at[:, 0:128], fb_v.at[0], load_sem.at[1]),
        pltpu.make_async_copy(fa.at[:, mir_lanes], fa_v.at[0], load_sem.at[2]),
        pltpu.make_async_copy(fa.at[:, own_lanes], fa_v.at[1], load_sem.at[3]),
        pltpu.make_async_copy(tau, tau_v, load_sem.at[4]),
    ] + [
        pltpu.make_async_copy(fb.at[:, t * 128 : (t + 1) * 128], fb_v.at[t], load_sem.at[4 + t])
        for t in range(1, 4)
    ]
    for load in loads:
        load.start()

    z_peers = [at(z_=(z + s) % NZ) for s in range(1, NZ)]
    x_peers = [at(x_=(x + s) % NX) for s in range(1, NX)]
    y_offsets = [(dh, dl) for dh in range(NH) for dl in range(NL) if (dh, dl) != (0, 0)]
    y_peers = [at(h_=(h + dh) % NH, l_=(l + dl) % NL) for dh, dl in y_offsets]
    sibling = at(k_=1 - k)
    barrier = pltpu.get_barrier_semaphore()
    everyone = z_peers + x_peers + y_peers + [sibling]
    for peer in everyone:
        pl.semaphore_signal(barrier, inc=1, device_id=peer, device_id_type=MESH)

    lane128 = lanes_of((1, 128))
    low = lane128 < 64

    pb = spread(sb[...], 8)
    pa = spread(sa[...], 16)
    loads[0].wait()
    for n in (1, 5, 6, 7):
        loads[n].wait()
    parts = [[] for _ in range(8)]
    for g in range(3):
        prod = jnp.dot(pb, fo_v[g * 128 : (g + 1) * 128, :], precision=HIGHEST)
        for b in range(8):
            parts[b].append(strided(fb_v, g * 64 + b, 8, 8) - prod[b * 8 : (b + 1) * 8])
    stacked = []
    for b in range(8):
        whole = jnp.concatenate(parts[b], axis=0)
        stacked.append(jnp.concatenate([whole[:, t * 128 : (t + 1) * 128] for t in range(4)], axis=0))
    quarter = lane128 % 64 < 32
    for bq in range(2):
        x0, x1, x2, x3 = stacked[bq * 4 : bq * 4 + 4]
        u0 = jnp.where(low, x0, pltpu.roll(x2, 64, 1))
        u2 = jnp.where(low, pltpu.roll(x0, 64, 1), x2)
        u1 = jnp.where(low, x1, pltpu.roll(x3, 64, 1))
        u3 = jnp.where(low, pltpu.roll(x1, 64, 1), x3)
        ys = [
            jnp.where(quarter, u0, pltpu.roll(u1, 32, 1)),
            jnp.where(quarter, pltpu.roll(u0, 96, 1), u1),
            jnp.where(quarter, u2, pltpu.roll(u3, 32, 1)),
            jnp.where(quarter, pltpu.roll(u2, 96, 1), u3),
        ]
        for tt in range(2):
            for j in range(4):
                y = ys[j]
                piece = jnp.concatenate(
                    [y[tt * 24 : tt * 24 + 24], y[(2 + tt) * 24 : (2 + tt) * 24 + 24]], axis=0
                )
                b1_send[tt * 4 + j, :, bq * 128 : (bq + 1) * 128] = piece.astype(BF16)

    pl.semaphore_wait(barrier, len(everyone))

    b1 = []
    for s in range(1, NZ):
        zt = (z + s) % NZ
        b1.append(remote(b1_send.at[zt], b1_recv.at[z], b1_ss.at[s], b1_rs.at[s], at(z_=zt)))
        b1[-1].start()
    b1_recv[z] = b1_send[z]

    def dress_a(which):
        half = [[], []]
        for g in range(3):
            lanes = pl.ds(pl.multiple_of((ml if which == 0 else l) * 128, 128), 128)
            prod = jnp.dot(pa, fo_v[g * 128 : (g + 1) * 128, lanes], precision=HIGHEST)
            rows = []
            for a in range(16):
                d = fa_v[which, pl.ds(g * 128 + a, 8, stride=16), :] - prod[a * 8 : (a + 1) * 8]
                rows.append(d)
            for ah in range(2):
                lane_tiles = []
                for pair in range(4):
                    d0, d1 = rows[ah * 8 + pair * 2], rows[ah * 8 + pair * 2 + 1]
                    r0, r1 = pltpu.roll(d0, 64, 1), pltpu.roll(d1, 64, 1)
                    e0 = jnp.where(k == 0, d0, r0)
                    e1 = jnp.where(k == 0, r1, d1)
                    lane_tiles.append(jnp.where(low, e0, e1))
                half[ah].append(jnp.concatenate(lane_tiles, axis=1))
        return jnp.concatenate(half[0] + half[1], axis=0).astype(BF16)

    loads[2].wait()
    a_mir[...] = dress_a(0)
    mirror = at(h_=1 - h, l_=ml)
    am = remote(a_mir, a_blk.at[z, h], am_ss.at[0], am_rs.at[0], mirror)
    am.start()
    loads[3].wait()
    a_blk[z, h] = dress_a(1)

    right, left = at(z_=(z + 1) % NZ), at(z_=(z + NZ - 1) % NZ)
    a_sent = []

    def a_send(way, step, part):
        zs = (z - step + NZ) % NZ if way == 0 else (z + step) % NZ
        hs = h if part == 0 else 1 - h
        ref = a_blk.at[zs, hs]
        n = step * 2 + part
        copy = remote(ref, ref, a_ss.at[way, n], a_rs.at[way, n], right if way == 0 else left)
        copy.start()
        a_sent.append(copy)

    def a_wait(way, step, part):
        zs = (z - step - 1 + NZ) % NZ if way == 0 else (z + step + 1) % NZ
        hs = h if part == 0 else 1 - h
        n = step * 2 + part
        wait_recv(a_blk.at[zs, hs], a_ss.at[way, n], a_rs.at[way, n])

    a_send(0, 0, 0)
    a_send(1, 0, 0)

    loads[4].wait()
    put(tf_v, tau_v[...].astype(F32))
    for d in range(8):
        for e in range(2):
            t_all[x, d * 64 + e * 32 : d * 64 + e * 32 + 32, :] = strided(
                tf_v, e * 256 + d, 32, 8
            ).astype(BF16)
    ts = []
    for s in range(1, NX):
        ref = t_all.at[x]
        ts.append(remote(ref, ref, t_ss.at[s], t_rs.at[s], at(x_=(x + s) % NX)))
        ts[-1].start()

    for s in range(1, NZ):
        wait_recv(b1_recv.at[(z - s + NZ) % NZ], b1_ss.at[s], b1_rs.at[s])
    ri, ci = rows_of((256, 256)), lanes_of((256, 256))
    perm = ((ri // 8 == ci % 32) & (ri % 8 == ci // 32)).astype(BF16)
    blocks = [b1_recv[zz].astype(F32) for zz in range(NZ)]
    for hd in range(NH):
        rows = [blk[hd * 24 : hd * 24 + 24] for blk in blocks] + [jnp.zeros((64, 256), F32)]
        stack = jnp.concatenate(rows, axis=0).astype(BF16)
        bt = lax.dot_general(perm, stack, (((1,), (1,)), ((), ())), preferred_element_type=F32)
        rest = bt[:, 128:]
        fold = jnp.where(low, rest[:128], pltpu.roll(rest[128:], 64, 1))
        b2_send[hd, 0:256] = bt[:, :128].astype(BF16)
        b2_send[hd, 256:384] = fold.astype(BF16)
    b2 = []
    for n, (dh, dl) in enumerate(y_offsets):
        hd, ld = (h + dh) % NH, (l + dl) % NL
        b2.append(
            remote(b2_send.at[hd], b_all.at[h, col], b2_ss.at[n], b2_rs.at[n], at(h_=hd, l_=ld))
        )
        b2[-1].start()
    fw = [remote(b2_send.at[h], b_all.at[h, col], fw_ss.at[7], fw_rs.at[7], sibling)]
    fw[0].start()
    b_all[h, col] = b2_send[h]

    wait_recv(a_blk.at[z, 1 - h], am_ss.at[0], am_rs.at[0])
    a_send(0, 0, 1)
    a_send(1, 0, 1)
    for step in range(3):
        for part in range(2):
            for way in range(2):
                a_wait(way, step, part)
                if step < 2 or way == part:
                    a_send(way, step + 1, part)

    for n, (dh, dl) in enumerate(y_offsets):
        hs, ls = (h + dh) % NH, (l - dl + NL) % NL
        ref = b_all.at[hs, col_id(ls, k)]
        wait_recv(ref, b2_ss.at[n], b2_rs.at[n])
        fw.append(remote(ref, ref, fw_ss.at[n], fw_rs.at[n], sibling))
        fw[-1].start()

    a_wait(0, 3, 0)
    a_wait(1, 3, 1)
    for zp in range(4):
        for hh in range(2):
            b0, b1_ = a_blk[2 * zp, hh].astype(F32), a_blk[2 * zp + 1, hh].astype(F32)
            for ah in range(2):
                both = jnp.concatenate([b0[ah * 24 : ah * 24 + 24], b1_[ah * 24 : ah * 24 + 24]], axis=0)
                both = both.astype(BF16)
                cols = slice(ah * 512, (ah + 1) * 512)
                r = zp * 48
                split = min(max(128 - r, 0), 48)
                if split > 0:
                    a_all[hh * 128 + r : hh * 128 + r + split, cols] = both[:split]
                if split < 48:
                    start = 256 + hh * 64 + r + split - 128
                    a_all[start : start + 48 - split, cols] = both[split:]

    wait_recv(b_all.at[h, col_id(l, 1 - k)], fw_ss.at[7], fw_rs.at[7])
    for n, (dh, dl) in enumerate(y_offsets):
        hs, ls = (h + dh) % NH, (l - dl + NL) % NL
        wait_recv(b_all.at[hs, col_id(ls, 1 - k)], fw_ss.at[n], fw_rs.at[n])
    for n in range(8):
        bt_all[n, :, 0:128] = b_all[0, n, 0:256]
        bt_all[n, :, 128:256] = b_all[1, n, 0:256]
        f0, f1 = b_all[0, n, 256:384].astype(F32), b_all[1, n, 256:384].astype(F32)
        bt_all[n, 0:128, 256:384] = jnp.where(low, f0, pltpu.roll(f1, 64, 1)).astype(BF16)
        bt_all[n, 128:256, 256:384] = jnp.where(low, pltpu.roll(f0, 64, 1), f1).astype(BF16)

    @pl.loop(0, 8)
    def _(i):
        lhs = bt_all[:, pl.ds(pl.multiple_of(i * 32, 32), 32), :].reshape(256, 384)
        prod = jnp.dot(lhs, a_all[...], preferred_element_type=F32)
        prod = prod.reshape(8, 4, 8, 1024)
        for pair in range(2):
            p0 = prod[:, 2 * pair].reshape(64, 1024)
            p1 = prod[:, 2 * pair + 1].reshape(64, 1024)
            lanes = pl.ds(pl.multiple_of(i * 256 + pair * 128, 128), 128)
            for j in range(8):
                q0, q1 = p0[:, j * 128 : (j + 1) * 128], p1[:, j * 128 : (j + 1) * 128]
                e = jnp.where(low, q0, pltpu.roll(q1, 64, 1)).astype(BF16)
                o = jnp.where(low, pltpu.roll(q0, 64, 1), q1).astype(BF16)
                row = ((j % 2) * 8 + (j // 2) * 2) * 64
                integral[row : row + 64, lanes] = e
                integral[row + 64 : row + 128, lanes] = o

    for s in range(1, NX):
        wait_recv(t_all.at[(x - s + NX) % NX], t_ss.at[s], t_rs.at[s])

    def contract(which):
        rows = pl.ds(pl.multiple_of(which * 512, 512), 512)
        total = jnp.zeros((512, 256), F32)
        for n in range(NX):
            total += jnp.dot(
                integral[rows, n * 512 : (n + 1) * 512], t_all[n], preferred_element_type=F32
            )
        return total

    put(acc_p, contract(1 - k))
    cs = []
    for n in range(NX):
        c_send[n] = strided(acc_p, n, 128, 4).astype(BF16)
        cs.append(remote(c_send.at[n], c_recv.at[n], c_ss.at[n], c_rs.at[n], sibling))
        cs[-1].start()
    put(acc_o, contract(k))
    for n in range(NX):
        wait_recv(c_recv.at[n], c_ss.at[n], c_rs.at[n])
    xs = []
    for s in range(1, NX):
        xt = (x + s) % NX
        value = strided(acc_o, xt, 128, 4) + c_recv[xt].astype(F32)
        x_send[s] = value.astype(BF16)
        xs.append(remote(x_send.at[s], x_recv.at[s], x_ss.at[s], x_rs.at[s], at(x_=xt)))
        xs[-1].start()
    own = strided(acc_o, x, 128, 4) + c_recv[x].astype(F32)
    for s in range(1, NX):
        wait_recv(x_recv.at[s], x_ss.at[s], x_rs.at[s])
        own += x_recv[s].astype(F32)
    put(s_v, own)
    zs_ = []
    for s in range(1, NZ):
        zt = (z + s) % NZ
        z_send[s] = strided(s_v, zt, 16, 8).astype(BF16)
        zs_.append(remote(z_send.at[s], z_recv.at[s], z_ss.at[s], z_rs.at[s], at(z_=zt)))
        zs_[-1].start()
    own = strided(s_v, z, 16, 8)
    for s in range(1, NZ):
        wait_recv(z_recv.at[s], z_ss.at[s], z_rs.at[s])
        own += z_recv[s].astype(F32)
    put(s2_v, own)
    ys_ = []
    for n, (dh, dl) in enumerate(y_offsets):
        hd, ld = (h + dh) % NH, (l + dl) % NL
        y_send[n] = strided(s2_v, ld * 4 + hd, 2, 2)
        ys_.append(remote(y_send.at[n], y_recv.at[n], y_ss.at[n], y_rs.at[n], at(h_=hd, l_=ld)))
        ys_[-1].start()
    pair = lanes_of((1, 256))
    energy = jnp.zeros((1, 256), F32)
    for n in range(16):
        energy += jnp.where(pair // 16 == n, oo[n], 0.0) + jnp.where(pair % 16 == n, oo[n], 0.0)
    own = strided(s2_v, l * 4 + h, 2, 2)
    for n in range(len(y_offsets)):
        wait_recv(y_recv.at[n], y_ss.at[n], y_rs.at[n])
        own += y_recv[n]
    for j in range(2):
        out[j] = own[j : j + 1] / (oa[j] + ob[0] - energy)

    for copy in b1 + [am] + a_sent + ts + b2 + fw + cs + xs + zs_ + ys_:
        copy.wait_send()


def body(fa, fb, fo, sa, sb, tau, oa, ob, oo):
    vmem = pl.BlockSpec(memory_space=pltpu.VMEM)
    smem = pl.BlockSpec(memory_space=pltpu.SMEM)
    hbm = pl.BlockSpec(memory_space=pl.ANY)
    dma = pltpu.SemaphoreType.DMA
    scratch = [
        pltpu.VMEM((384, 512), F32),
        pltpu.VMEM((4, 192, 128), F32),
        pltpu.VMEM((2, 384, 128), F32),
        pltpu.VMEM((512, 256), BF16),
        pltpu.VMEM((2, 512, 128), F32),
        pltpu.VMEM((8, 48, 256), BF16),
        pltpu.VMEM((8, 48, 256), BF16),
        pltpu.VMEM((2, 384, 128), BF16),
        pltpu.VMEM((2, 8, 384, 128), BF16),
        pltpu.VMEM((8, 256, 384), BF16),
        pltpu.VMEM((8, 2, 48, 512), BF16),
        pltpu.VMEM((48, 512), BF16),
        pltpu.VMEM((384, 1024), BF16),
        pltpu.VMEM((4, 512, 256), BF16),
        pltpu.VMEM((1024, 2048), BF16),
        pltpu.VMEM((2, 512, 128), F32),
        pltpu.VMEM((2, 512, 128), F32),
        pltpu.VMEM((4, 128, 256), BF16),
        pltpu.VMEM((4, 128, 256), BF16),
        pltpu.VMEM((4, 128, 256), BF16),
        pltpu.VMEM((4, 128, 256), BF16),
        pltpu.VMEM((2, 128, 128), F32),
        pltpu.VMEM((8, 16, 256), BF16),
        pltpu.VMEM((8, 16, 256), BF16),
        pltpu.VMEM((2, 16, 128), F32),
        pltpu.VMEM((8, 2, 256), F32),
        pltpu.VMEM((8, 2, 256), F32),
        dma((8,)),
        dma((8,)), dma((8,)),
        dma((8,)), dma((8,)),
        dma((8,)), dma((8,)),
        dma((1,)), dma((1,)),
        dma((2, 8)), dma((2, 8)),
        dma((4,)), dma((4,)),
        dma((4,)), dma((4,)),
        dma((4,)), dma((4,)),
        dma((8,)), dma((8,)),
        dma((8,)), dma((8,)),
    ]
    return pl.pallas_call(
        kernel,
        out_shape=jax.ShapeDtypeStruct((2, 1, 256), F32),
        in_specs=[hbm, hbm, hbm, vmem, vmem, hbm, smem, smem, smem],
        out_specs=vmem,
        scratch_shapes=scratch,
        compiler_params=pltpu.CompilerParams(
            collective_id=0, has_side_effects=True, vmem_limit_bytes=60 * 1024 * 1024
        ),
        name="ladder",
    )(
        fa.reshape(384, 512),
        fb.reshape(192, 512),
        fo.reshape(384, 512),
        sa,
        sb,
        tau.reshape(512, 256),
        oa,
        ob,
        oo,
    )


def solution(mesh):
    return jax.shard_map(
        body,
        mesh=mesh,
        in_specs=(
            P("dev", None, None),
            P("dev", "col", None),
            P("dev", None, None),
            P(),
            P(None, "col"),
            P("col", "dev", None),
            P("col"),
            P("dev"),
            P(),
        ),
        out_specs=P("col", "dev", None),
        check_vma=False,
    )
```

```python
import jax
import jax.numpy as jnp
from jax import lax
from jax.experimental import pallas as pl
from jax.experimental.pallas import tpu as pltpu
from jax.sharding import PartitionSpec as P

MESH = pl.DeviceIdType.MESH
F32 = jnp.float32
BF16 = jnp.bfloat16
HIGHEST = lax.Precision.HIGHEST
NH, NZ, NX, NL, NK = 2, 8, 4, 4, 2


def lanes_of(shape):
    return lax.broadcasted_iota(jnp.int32, shape, len(shape) - 1)


def rows_of(shape):
    return lax.broadcasted_iota(jnp.int32, shape, 0)


def spread(singles, rows):
    pick = (rows_of((rows * 8, rows)) // 8 == lanes_of((rows * 8, rows))).astype(F32)
    across = (rows_of((16, 128)) == lanes_of((16, 128)) % 16).astype(F32)
    first = lax.dot_general(pick, singles, (((1,), (0,)), ((), ())), precision=HIGHEST)
    full = jnp.dot(first, across, precision=HIGHEST)
    same = rows_of((rows * 8, 128)) % 8 == lanes_of((rows * 8, 128)) // 16
    return jnp.where(same, full, 0.0)


def strided(ref, start, size, stride):
    tiles = [ref[t, pl.ds(start, size, stride=stride), :] for t in range(ref.shape[0])]
    return jnp.concatenate(tiles, axis=1)


def put(ref, value):
    for t in range(ref.shape[0]):
        ref[t] = value[:, t * 128 : (t + 1) * 128]


def kernel(
    fa, fb, fo, sa, sb, tau, oa, ob, oo, out,
    fo_v, fb_v, fa_v, tau_v, tf_v,
    b1_send, b1_recv, b2_send, b_all,
    a_blk, a_mir, a_all, t_all, integral, acc,
    c_send, c_recv, x_send, x_recv, s_v, z_send, z_recv, s2_v, y_recv,
    load_sem, b1_ss, b1_rs, b2_ss, b2_rs, rl_ss, rl_rs, fw_ss, fw_rs, am_ss, am_rs, a_ss, a_rs,
    t_ss, t_rs, c_ss, c_rs, x_ss, x_rs, z_ss, z_rs, y_ss, y_rs,
):
    col = lax.axis_index("col")
    dev = lax.axis_index("dev")
    l, k = col // NK, col % NK
    h, z, x = dev // (NZ * NX), (dev // NX) % NZ, dev % NX
    sent = []

    def col_id(l_, k_):
        return l_ * NK + k_

    def at(h_=h, z_=z, x_=x, l_=l, k_=k):
        return (col_id(l_, k_), (h_ * NZ + z_) * NX + x_)

    def remote(src, dst, ss, rs, target):
        return pltpu.make_async_remote_copy(
            src_ref=src, dst_ref=dst, send_sem=ss, recv_sem=rs, device_id=target, device_id_type=MESH
        )

    def send(src, dst, ss, rs, target):
        copy = remote(src, dst, ss, rs, target)
        copy.start()
        sent.append(copy)

    def flush():
        while sent:
            sent.pop().wait_send()

    sibling = at(k_=1 - k)

    def wait_recv(dst, ss, rs):
        remote(dst, dst, ss, rs, sibling).wait_recv()

    ml = NL - 1 - l
    own_lanes = pl.ds(pl.multiple_of(l * 128, 128), 128)
    mir_lanes = pl.ds(pl.multiple_of(ml * 128, 128), 128)
    loads = [
        pltpu.make_async_copy(fo, fo_v, load_sem.at[0]),
        pltpu.make_async_copy(fa.at[:, mir_lanes], fa_v.at[0], load_sem.at[5]),
        pltpu.make_async_copy(fa.at[:, own_lanes], fa_v.at[1], load_sem.at[6]),
        pltpu.make_async_copy(tau, tau_v, load_sem.at[7]),
    ]
    loads[1:1] = [
        pltpu.make_async_copy(fb.at[:, t * 128 : (t + 1) * 128], fb_v.at[t], load_sem.at[1 + t])
        for t in range(4)
    ]
    for load in loads:
        load.start()

    y_offsets = [(e, f) for e in range(NH) for f in range(NL) if (e, f) != (0, 0)]
    everyone = [at(z_=(z + s) % NZ) for s in range(1, NZ)]
    everyone += [at(x_=(x + s) % NX) for s in range(1, NX)]
    everyone += [at(h_=(h + e) % NH, l_=(l + f) % NL) for e, f in y_offsets]
    everyone += [sibling]
    barrier = pltpu.get_barrier_semaphore()
    for peer in everyone:
        pl.semaphore_signal(barrier, inc=1, device_id=peer, device_id_type=MESH)

    lane128 = lanes_of((1, 128))
    low = lane128 < 64
    low16 = lanes_of((16, 128)) < 64

    pb = spread(sb[...], 8)
    for load in loads[:5]:
        load.wait()
    parts = [[] for _ in range(8)]
    for g in range(3):
        prod = jnp.dot(pb, fo_v[g * 128 : (g + 1) * 128, :], precision=HIGHEST)
        for b in range(8):
            parts[b].append(strided(fb_v, g * 64 + b, 8, 8) - prod[b * 8 : (b + 1) * 8])
    stacked = []
    for b in range(8):
        whole = jnp.concatenate(parts[b], axis=0)
        stacked.append(jnp.concatenate([whole[:, t * 128 : (t + 1) * 128] for t in range(4)], axis=0))
    quarter = lane128 % 64 < 32
    eighth = lane128 % 32 < 16
    ys = []
    for bq in range(2):
        x0, x1, x2, x3 = stacked[bq * 4 : bq * 4 + 4]
        u0 = jnp.where(low, x0, pltpu.roll(x2, 64, 1))
        u2 = jnp.where(low, pltpu.roll(x0, 64, 1), x2)
        u1 = jnp.where(low, x1, pltpu.roll(x3, 64, 1))
        u3 = jnp.where(low, pltpu.roll(x1, 64, 1), x3)
        ys.append([
            jnp.where(quarter, u0, pltpu.roll(u1, 32, 1)),
            jnp.where(quarter, pltpu.roll(u0, 96, 1), u1),
            jnp.where(quarter, u2, pltpu.roll(u3, 32, 1)),
            jnp.where(quarter, pltpu.roll(u2, 96, 1), u3),
        ])
    for j in range(4):
        y0, y1 = ys[0][j], ys[1][j]
        halves = (
            jnp.where(eighth, y0, pltpu.roll(y1, 16, 1)),
            jnp.where(eighth, pltpu.roll(y0, 112, 1), y1),
        )
        for c in range(2):
            for tt in range(2):
                y = halves[c]
                piece = jnp.concatenate(
                    [y[tt * 24 : tt * 24 + 24], y[(2 + tt) * 24 : (2 + tt) * 24 + 24]], axis=0
                )
                b1_send[c, tt * 4 + j] = piece.astype(BF16)

    pl.semaphore_wait(barrier, len(everyone))

    for c in range(2):
        for s in range(1, NZ):
            zt = (z + s) % NZ
            send(b1_send.at[c, zt], b1_recv.at[c, z], b1_ss.at[c, s], b1_rs.at[c, s], at(z_=zt))
        b1_recv[c, z] = b1_send[c, z]

    pa = spread(sa[...].T, 16)

    def dress_a(which):
        half = [[], []]
        for g in range(3):
            lanes = mir_lanes if which == 0 else own_lanes
            prod = jnp.dot(pa, fo_v[g * 128 : (g + 1) * 128, lanes], precision=HIGHEST)
            rows = []
            for a in range(16):
                d = fa_v[which, pl.ds(g * 128 + a, 8, stride=16), :] - prod[a * 8 : (a + 1) * 8]
                rows.append(d)
            for ah in range(2):
                lane_tiles = []
                for pair in range(4):
                    d0, d1 = rows[ah * 8 + pair * 2], rows[ah * 8 + pair * 2 + 1]
                    r0, r1 = pltpu.roll(d0, 64, 1), pltpu.roll(d1, 64, 1)
                    e0 = jnp.where(k == 0, d0, r0)
                    e1 = jnp.where(k == 0, r1, d1)
                    lane_tiles.append(jnp.where(low, e0, e1))
                half[ah].append(jnp.concatenate(lane_tiles, axis=1))
        return jnp.concatenate(half[0] + half[1], axis=0).astype(BF16)

    kinds = [1, -1, 2, -2, 3, -3, 4]

    def a_send(source, part, kind, by):
        ref = a_blk.at[source % NZ, h if part == 0 else 1 - h]
        n = kinds.index(kind)
        send(ref, ref, a_ss.at[part, n], a_rs.at[part, n], at(z_=(z + by + NZ) % NZ))

    def a_wait(part, kind):
        ref = a_blk.at[(z - kind + NZ) % NZ, h if part == 0 else 1 - h]
        n = kinds.index(kind)
        wait_recv(ref, a_ss.at[part, n], a_rs.at[part, n])

    def a_first(part):
        for kind in (2, -2, 1, -1):
            a_send(z, part, kind, kind)

    def a_second(part):
        a_wait(part, 2)
        a_send(z - 2 + NZ, part, 3, 1)
        if part == 0:
            a_send(z - 2 + NZ, part, 4, 2)
        a_wait(part, -2)
        a_send(z + 2, part, -3, -1)
        if part == 1:
            a_send(z + 2, part, 4, -2)

    loads[5].wait()
    a_mir[...] = dress_a(0)
    send(a_mir, a_blk.at[z, h], am_ss.at[0], am_rs.at[0], at(h_=1 - h, l_=ml))
    loads[6].wait()
    a_blk[z, h] = dress_a(1)
    a_first(0)

    loads[7].wait()
    put(tf_v, tau_v[...].astype(F32))
    for d in range(8):
        for e in range(2):
            t_all[x, d * 64 + e * 32 : d * 64 + e * 32 + 32, :] = strided(
                tf_v, e * 256 + d, 32, 8
            ).astype(BF16)
    for s in range(1, NX):
        ref = t_all.at[x]
        send(ref, ref, t_ss.at[s], t_rs.at[s], at(x_=(x + s) % NX))

    ri, ci = rows_of((128, 128)), lanes_of((128, 128))
    perm = ((ri // 8 == ci % 16) & (ri % 8 == (ci % 32) // 16 * 4 + ci // 32)).astype(BF16)

    def b_second(c):
        for s in range(1, NZ):
            wait_recv(b1_recv.at[c, (z - s + NZ) % NZ], b1_ss.at[c, s], b1_rs.at[c, s])
        blocks = [b1_recv[c, zz].astype(F32) for zz in range(NZ)]
        for hd in range(NH):
            rows = [blk[hd * 24 : hd * 24 + 24] for blk in blocks] + [jnp.zeros((64, 128), F32)]
            stack = jnp.concatenate(rows, axis=0).astype(BF16)
            bt = lax.dot_general(perm, stack, (((1,), (1,)), ((), ())), preferred_element_type=F32)
            rest = bt[:, 128:]
            fold = jnp.where(low, rest[:64], pltpu.roll(rest[64:], 64, 1))
            b2_send[c, hd, 0:128] = bt[:, :128].astype(BF16)
            b2_send[c, hd, 128:192] = fold.astype(BF16)
        for n, (hd, ld) in enumerate([(h, 2 - p), (h, partner), (1 - h, i0), (1 - h, 3 - i3)]):
            slot = (n // 2) * NL + l
            target = at(h_=hd, l_=ld)
            send(b2_send.at[c, hd], b_all.at[c, h, col], b2_ss.at[c, n], b2_rs.at[c, slot], target)
        send(b2_send.at[c, h], b_all.at[c, h, col], fw_ss.at[c, 0], fw_rs.at[c, l], sibling)
        b_all[c, h, col] = b2_send[c, h]

    p = l // 2
    partner = l + 1 - 2 * (l % 2)
    i0, i3 = (NL - 1 - l) // 3, l // 3

    def direct(l_):
        outer = ((l_ + 1) // 2 + 1) % 2
        right = l_ // 2
        named = []
        for n in range(3):
            left = outer * (3 - n) + (1 - outer) * (2, 3, 0)[n]
            half = outer + (1 - outer) * (0, 0, 1)[n]
            named.append((half, left * (1 - right) + (3 - left) * right))
        return named

    def b_block(c, name, k_):
        return b_all.at[c, (h + name[0]) % NH, col_id(name[1], k_)]

    def b_forward(c, name, n):
        ref = b_block(c, name, k)
        send(ref, ref, fw_ss.at[c, n], fw_rs.at[c, name[0] * NL + name[1]], sibling)

    def b_direct(c):
        for n, name in enumerate([(0, partner)] + direct(l)):
            ref = b_block(c, name, k)
            slot = name[0] * NL + name[1]
            wait_recv(ref, b2_ss.at[c, 0], b2_rs.at[c, slot])
            if n > 0:
                send(ref, ref, rl_ss.at[c, n], rl_rs.at[c, slot], at(l_=partner))
            b_forward(c, name, 1 + n)

    def b_relayed(c):
        for n, name in enumerate(direct(partner)):
            slot = name[0] * NL + name[1]
            wait_recv(b_block(c, name, k), rl_ss.at[c, 0], rl_rs.at[c, slot])
            b_forward(c, name, 5 + n)

    def b_forwarded(c):
        for half in range(NH):
            for l_ in range(NL):
                wait_recv(b_block(c, (half, l_), 1 - k), fw_ss.at[c, 0], fw_rs.at[c, half * NL + l_])

    b_second(0)
    b_second(1)
    wait_recv(a_blk.at[z, 1 - h], am_ss.at[0], am_rs.at[0])
    a_first(1)
    b_direct(0)
    a_second(0)
    b_relayed(0)
    a_second(1)
    b_direct(1)
    for part in range(2):
        for kind in (1, -1, 3, -3, 4):
            a_wait(part, kind)
    for zp in range(4):
        for hh in range(2):
            b0, b1 = a_blk[2 * zp, hh].astype(F32), a_blk[2 * zp + 1, hh].astype(F32)
            for ah in range(2):
                both = jnp.concatenate([b0[ah * 24 : ah * 24 + 24], b1[ah * 24 : ah * 24 + 24]], axis=0)
                both = both.astype(BF16)
                cols = slice(ah * 512, (ah + 1) * 512)
                r = zp * 48
                split = min(max(128 - r, 0), 48)
                if split > 0:
                    a_all[hh * 128 + r : hh * 128 + r + split, cols] = both[:split]
                if split < 48:
                    start = 256 + hh * 64 + r + split - 128
                    a_all[start : start + 48 - split, cols] = both[split:]

    def unit(c, u):
        rows = []
        for g in range(2):
            lg = 2 * u + g
            for kk in range(NK):
                m = col_id(lg, kk)
                m0, m1 = b_all[c, 0, m, 0:128], b_all[c, 1, m, 0:128]
                f0, f1 = b_all[c, 0, m, 128:192].astype(F32), b_all[c, 1, m, 128:192].astype(F32)
                top = jnp.where(low, f0, pltpu.roll(f1, 64, 1))
                bottom = jnp.where(low, pltpu.roll(f0, 64, 1), f1)
                rest = jnp.concatenate([top, bottom], axis=0).astype(BF16)
                rows.append(jnp.concatenate([m0, m1, rest], axis=1))
        lhs = jnp.concatenate(rows, axis=0)
        for jj in range(4):
            whole = jnp.dot(lhs, a_all[:, jj * 256 : (jj + 1) * 256], preferred_element_type=F32)
            for j in (2 * jj, 2 * jj + 1):
                for g in range(2):
                    prod = whole[g * 256 : (g + 1) * 256, (j % 2) * 128 : (j % 2) * 128 + 128]
                    prod = prod.reshape(2, 16, 8, 128)
                    row = g * 256 + (j % 2) * 128 + (j // 2) * 32
                    for i in range(8):
                        q0 = prod[:, 2 * i].reshape(16, 128).astype(BF16)
                        q1 = prod[:, 2 * i + 1].reshape(16, 128).astype(BF16)
                        e = jnp.where(low16, q0, pltpu.roll(q1, 64, 1))
                        o = jnp.where(low16, pltpu.roll(q0, 64, 1), q1)
                        integral[row : row + 16, i * 128 : (i + 1) * 128] = e
                        integral[row + 16 : row + 32, i * 128 : (i + 1) * 128] = o
        total = jnp.dot(integral[:, 0:512], t_all[2 * c], preferred_element_type=F32)
        total += jnp.dot(integral[:, 512:1024], t_all[2 * c + 1], preferred_element_type=F32)
        for g in range(2):
            for t in range(2):
                part = total[g * 256 : (g + 1) * 256, t * 128 : (t + 1) * 128]
                acc[2 * u + g, t] = part if c == 0 else acc[2 * u + g, t] + part

    for s in range(1, NX):
        wait_recv(t_all.at[(x - s + NX) % NX], t_ss.at[s], t_rs.at[s])
    b_forwarded(0)
    unit(0, 0)
    b_relayed(1)
    unit(0, 1)
    b_forwarded(1)

    def mine(u, half, x_):
        return jnp.concatenate([strided(acc.at[2 * u + g], half * 128 + x_, 32, 4) for g in range(2)], axis=0)

    def core_send(u):
        for x_ in range(NX):
            c_send[u, x_] = mine(u, 1 - k, x_).astype(BF16)
        send(c_send.at[u], c_recv.at[u], c_ss.at[u], c_rs.at[u], sibling)

    def x_exchange(u):
        wait_recv(c_recv.at[u], c_ss.at[u], c_rs.at[u])
        for n in range(1, NX):
            x_ = (x + n) % NX
            x_send[u, n] = (mine(u, k, x_) + c_recv[u, x_].astype(F32)).astype(BF16)
            send(x_send.at[u, n], x_recv.at[u, n], x_ss.at[u, n], x_rs.at[u, n], at(x_=x_))

    def x_sum(u):
        own = mine(u, k, x) + c_recv[u, x].astype(F32)
        for n in range(1, NX):
            wait_recv(x_recv.at[u, n], x_ss.at[u, n], x_rs.at[u, n])
            own += x_recv[u, n].astype(F32)
        for g in range(2):
            put(s_v.at[2 * u + g], own[g * 32 : g * 32 + 32])

    unit(1, 0)
    core_send(0)
    unit(1, 1)
    core_send(1)
    flush()
    x_exchange(0)
    x_exchange(1)
    x_sum(0)
    x_sum(1)

    def rows_for(z_):
        both = [strided(s_v.at[2 * half + z_ // 4], z_ % 4, 8, 4) for half in range(NH)]
        return jnp.concatenate(both, axis=0)

    for n in range(1, NZ):
        z_ = (z + n) % NZ
        z_send[n] = rows_for(z_).astype(BF16)
        send(z_send.at[n], z_recv.at[n], z_ss.at[n], z_rs.at[n], at(z_=z_))
    own = rows_for(z)
    flush()
    for n in range(1, NZ):
        wait_recv(z_recv.at[n], z_ss.at[n], z_rs.at[n])
        own += z_recv[n].astype(F32)
    for n in range(8):
        s2_v[n] = own[2 * n : 2 * n + 2]
    for n, (e, f) in enumerate(y_offsets):
        h_, l_ = (h + e) % NH, (l + f) % NL
        send(s2_v.at[h_ * NL + l_], y_recv.at[n], y_ss.at[n], y_rs.at[n], at(h_=h_, l_=l_))
    lane256 = lanes_of((1, 256))
    energy = jnp.zeros((1, 256), F32)
    for n in range(16):
        energy += jnp.where(lane256 // 16 == n, oo[n], 0.0) + jnp.where(lane256 % 16 == n, oo[n], 0.0)
    own = s2_v[h * NL + l]
    for n in range(len(y_offsets)):
        wait_recv(y_recv.at[n], y_ss.at[n], y_rs.at[n])
        own += y_recv[n]
    for j in range(2):
        out[j] = own[j : j + 1] / (oa[j] + ob[0] - energy)

    flush()


def body(fa, fb, fo, sa, sb, tau, oa, ob, oo):
    vmem = pl.BlockSpec(memory_space=pltpu.VMEM)
    smem = pl.BlockSpec(memory_space=pltpu.SMEM)
    hbm = pl.BlockSpec(memory_space=pl.ANY)
    dma = pltpu.SemaphoreType.DMA
    scratch = [
        pltpu.VMEM((384, 512), F32),
        pltpu.VMEM((4, 192, 128), F32),
        pltpu.VMEM((2, 384, 128), F32),
        pltpu.VMEM((512, 256), BF16),
        pltpu.VMEM((2, 512, 128), F32),
        pltpu.VMEM((2, 8, 48, 128), BF16),
        pltpu.VMEM((2, 8, 48, 128), BF16),
        pltpu.VMEM((2, 2, 192, 128), BF16),
        pltpu.VMEM((2, 2, 8, 192, 128), BF16),
        pltpu.VMEM((8, 2, 48, 512), BF16),
        pltpu.VMEM((48, 512), BF16),
        pltpu.VMEM((384, 1024), BF16),
        pltpu.VMEM((4, 512, 256), BF16),
        pltpu.VMEM((512, 1024), BF16),
        pltpu.VMEM((4, 2, 256, 128), F32),
        pltpu.VMEM((2, 4, 64, 256), BF16),
        pltpu.VMEM((2, 4, 64, 256), BF16),
        pltpu.VMEM((2, 4, 64, 256), BF16),
        pltpu.VMEM((2, 4, 64, 256), BF16),
        pltpu.VMEM((4, 2, 32, 128), F32),
        pltpu.VMEM((8, 16, 256), BF16),
        pltpu.VMEM((8, 16, 256), BF16),
        pltpu.VMEM((8, 2, 256), F32),
        pltpu.VMEM((8, 2, 256), F32),
        dma((8,)),
        dma((2, 8)), dma((2, 8)),
        dma((2, 8)), dma((2, 8)),
        dma((2, 8)), dma((2, 8)),
        dma((2, 8)), dma((2, 8)),
        dma((1,)), dma((1,)),
        dma((2, 7)), dma((2, 7)),
        dma((4,)), dma((4,)),
        dma((2,)), dma((2,)),
        dma((2, 4)), dma((2, 4)),
        dma((8,)), dma((8,)),
        dma((8,)), dma((8,)),
    ]
    return pl.pallas_call(
        kernel,
        out_shape=jax.ShapeDtypeStruct((2, 1, 256), F32),
        in_specs=[hbm, hbm, hbm, vmem, vmem, hbm, smem, smem, smem],
        out_specs=vmem,
        scratch_shapes=scratch,
        compiler_params=pltpu.CompilerParams(
            collective_id=0, has_side_effects=True, vmem_limit_bytes=60 * 1024 * 1024
        ),
        name="ladder",
    )(
        fa.reshape(384, 512),
        fb.reshape(192, 512),
        fo.reshape(384, 512),
        sa,
        sb.T,
        tau.reshape(512, 256),
        oa,
        ob,
        oo,
    )


def solution(mesh):
    return jax.shard_map(
        body,
        mesh=mesh,
        in_specs=(
            P("dev", None, None),
            P("dev", "col", None),
            P("dev", None, None),
            P(),
            P(None, "col"),
            P("col", "dev", None),
            P("col"),
            P("dev"),
            P(),
        ),
        out_specs=P("col", "dev", None),
        check_vma=False,
    )
```

```python
import jax
import jax.numpy as jnp
from jax import lax
from jax.experimental import pallas as pl
from jax.experimental.pallas import tpu as pltpu
from jax.sharding import PartitionSpec as P

MESH = pl.DeviceIdType.MESH
F32 = jnp.float32
BF16 = jnp.bfloat16
HIGHEST = lax.Precision.HIGHEST
NH, NZ, NX, NL, NK = 2, 8, 4, 4, 2


def lanes_of(shape):
    return lax.broadcasted_iota(jnp.int32, shape, len(shape) - 1)


def rows_of(shape):
    return lax.broadcasted_iota(jnp.int32, shape, 0)


def spread(singles, rows):
    pick = (rows_of((rows * 8, rows)) // 8 == lanes_of((rows * 8, rows))).astype(F32)
    across = (rows_of((16, 128)) == lanes_of((16, 128)) % 16).astype(F32)
    first = lax.dot_general(pick, singles, (((1,), (0,)), ((), ())), precision=HIGHEST)
    full = jnp.dot(first, across, precision=HIGHEST)
    same = rows_of((rows * 8, 128)) % 8 == lanes_of((rows * 8, 128)) // 16
    return jnp.where(same, full, 0.0)


def strided(ref, start, size, stride):
    tiles = [ref[t, pl.ds(start, size, stride=stride), :] for t in range(ref.shape[0])]
    return jnp.concatenate(tiles, axis=1)


def put(ref, value):
    for t in range(ref.shape[0]):
        ref[t] = value[:, t * 128 : (t + 1) * 128]


def kernel(
    fa, fb, fo, sa, sb, tau, oa, ob, oo, out,
    fo_v, fb_v, fa_v, tau_v, tf_v,
    b1_send, b1_recv, b2_send, b_all,
    a_blk, a_mir, a_all, t_all, integral, acc,
    c_send, c_recv, x_send, x_recv, s_v, z_send, z_recv, s2_v, y_recv,
    load_sem, b1_ss, b1_rs, b2_ss, b2_rs, fw_ss, fw_rs, am_ss, am_rs, a_ss, a_rs,
    t_ss, t_rs, c_ss, c_rs, x_ss, x_rs, z_ss, z_rs, y_ss, y_rs,
):
    col = lax.axis_index("col")
    dev = lax.axis_index("dev")
    l, k = col // NK, col % NK
    h, z, x = dev // (NZ * NX), (dev // NX) % NZ, dev % NX
    sent = []

    def col_id(l_, k_):
        return l_ * NK + k_

    def at(h_=h, z_=z, x_=x, l_=l, k_=k):
        return (col_id(l_, k_), (h_ * NZ + z_) * NX + x_)

    def remote(src, dst, ss, rs, target):
        return pltpu.make_async_remote_copy(
            src_ref=src, dst_ref=dst, send_sem=ss, recv_sem=rs, device_id=target, device_id_type=MESH
        )

    def send(src, dst, ss, rs, target):
        copy = remote(src, dst, ss, rs, target)
        copy.start()
        sent.append(copy)

    def flush():
        while sent:
            sent.pop().wait_send()

    sibling = at(k_=1 - k)

    def wait_recv(dst, ss, rs):
        remote(dst, dst, ss, rs, sibling).wait_recv()

    ml = NL - 1 - l
    own_lanes = pl.ds(pl.multiple_of(l * 128, 128), 128)
    mir_lanes = pl.ds(pl.multiple_of(ml * 128, 128), 128)
    loads = [
        pltpu.make_async_copy(fo, fo_v, load_sem.at[0]),
        pltpu.make_async_copy(fa.at[:, mir_lanes], fa_v.at[0], load_sem.at[5]),
        pltpu.make_async_copy(fa.at[:, own_lanes], fa_v.at[1], load_sem.at[6]),
        pltpu.make_async_copy(tau, tau_v, load_sem.at[7]),
    ]
    loads[1:1] = [
        pltpu.make_async_copy(fb.at[:, t * 128 : (t + 1) * 128], fb_v.at[t], load_sem.at[1 + t])
        for t in range(4)
    ]
    for load in loads:
        load.start()

    y_offsets = [(e, f) for e in range(NH) for f in range(NL) if (e, f) != (0, 0)]
    everyone = [at(z_=(z + s) % NZ) for s in range(1, NZ)]
    everyone += [at(x_=(x + s) % NX) for s in range(1, NX)]
    everyone += [at(h_=(h + e) % NH, l_=(l + f) % NL) for e, f in y_offsets]
    everyone += [sibling]
    barrier = pltpu.get_barrier_semaphore()
    for peer in everyone:
        pl.semaphore_signal(barrier, inc=1, device_id=peer, device_id_type=MESH)

    lane128 = lanes_of((1, 128))
    low = lane128 < 64
    low16 = lanes_of((16, 128)) < 64

    pb = spread(sb[...], 8)
    for load in loads[:5]:
        load.wait()
    parts = [[] for _ in range(8)]
    for g in range(3):
        prod = jnp.dot(pb, fo_v[g * 128 : (g + 1) * 128, :], precision=HIGHEST)
        for b in range(8):
            parts[b].append(strided(fb_v, g * 64 + b, 8, 8) - prod[b * 8 : (b + 1) * 8])
    stacked = []
    for b in range(8):
        whole = jnp.concatenate(parts[b], axis=0)
        stacked.append(jnp.concatenate([whole[:, t * 128 : (t + 1) * 128] for t in range(4)], axis=0))
    quarter = lane128 % 64 < 32
    eighth = lane128 % 32 < 16
    ys = []
    for bq in range(2):
        x0, x1, x2, x3 = stacked[bq * 4 : bq * 4 + 4]
        u0 = jnp.where(low, x0, pltpu.roll(x2, 64, 1))
        u2 = jnp.where(low, pltpu.roll(x0, 64, 1), x2)
        u1 = jnp.where(low, x1, pltpu.roll(x3, 64, 1))
        u3 = jnp.where(low, pltpu.roll(x1, 64, 1), x3)
        ys.append([
            jnp.where(quarter, u0, pltpu.roll(u1, 32, 1)),
            jnp.where(quarter, pltpu.roll(u0, 96, 1), u1),
            jnp.where(quarter, u2, pltpu.roll(u3, 32, 1)),
            jnp.where(quarter, pltpu.roll(u2, 96, 1), u3),
        ])
    for j in range(4):
        y0, y1 = ys[0][j], ys[1][j]
        halves = (
            jnp.where(eighth, y0, pltpu.roll(y1, 16, 1)),
            jnp.where(eighth, pltpu.roll(y0, 112, 1), y1),
        )
        for c in range(2):
            for tt in range(2):
                y = halves[c]
                piece = jnp.concatenate(
                    [y[tt * 24 : tt * 24 + 24], y[(2 + tt) * 24 : (2 + tt) * 24 + 24]], axis=0
                )
                b1_send[c, tt * 4 + j] = piece.astype(BF16)

    pl.semaphore_wait(barrier, len(everyone))

    for c in range(2):
        for s in range(1, NZ):
            zt = (z + s) % NZ
            send(b1_send.at[c, zt], b1_recv.at[c, z], b1_ss.at[c, s], b1_rs.at[c, s], at(z_=zt))
        b1_recv[c, z] = b1_send[c, z]

    pa = spread(sa[...].T, 16)

    def dress_a(which):
        half = [[], []]
        for g in range(3):
            lanes = mir_lanes if which == 0 else own_lanes
            prod = jnp.dot(pa, fo_v[g * 128 : (g + 1) * 128, lanes], precision=HIGHEST)
            rows = []
            for a in range(16):
                d = fa_v[which, pl.ds(g * 128 + a, 8, stride=16), :] - prod[a * 8 : (a + 1) * 8]
                rows.append(d)
            for ah in range(2):
                lane_tiles = []
                for pair in range(4):
                    d0, d1 = rows[ah * 8 + pair * 2], rows[ah * 8 + pair * 2 + 1]
                    r0, r1 = pltpu.roll(d0, 64, 1), pltpu.roll(d1, 64, 1)
                    e0 = jnp.where(k == 0, d0, r0)
                    e1 = jnp.where(k == 0, r1, d1)
                    lane_tiles.append(jnp.where(low, e0, e1))
                half[ah].append(jnp.concatenate(lane_tiles, axis=1))
        return jnp.concatenate(half[0] + half[1], axis=0).astype(BF16)

    kinds = [1, -1, 2, -2, 3, -3, 4]

    def a_send(source, part, kind, by):
        ref = a_blk.at[source % NZ, h if part == 0 else 1 - h]
        n = kinds.index(kind)
        send(ref, ref, a_ss.at[part, n], a_rs.at[part, n], at(z_=(z + by + NZ) % NZ))

    def a_wait(part, kind):
        ref = a_blk.at[(z - kind + NZ) % NZ, h if part == 0 else 1 - h]
        n = kinds.index(kind)
        wait_recv(ref, a_ss.at[part, n], a_rs.at[part, n])

    def a_first(part):
        for kind in (2, -2, 1, -1) if part == 0 else kinds:
            a_send(z, part, kind, kind)

    def a_second():
        a_wait(0, 2)
        a_send(z - 2 + NZ, 0, 3, 1)
        a_send(z - 2 + NZ, 0, 4, 2)
        a_wait(0, -2)
        a_send(z + 2, 0, -3, -1)

    loads[5].wait()
    a_mir[...] = dress_a(0)
    send(a_mir, a_blk.at[z, h], am_ss.at[0], am_rs.at[0], at(h_=1 - h, l_=ml))
    loads[6].wait()
    a_blk[z, h] = dress_a(1)
    a_first(0)

    loads[7].wait()
    put(tf_v, tau_v[...].astype(F32))
    for d in range(8):
        for e in range(2):
            t_all[x, d * 64 + e * 32 : d * 64 + e * 32 + 32, :] = strided(
                tf_v, e * 256 + d, 32, 8
            ).astype(BF16)
    for s in range(1, NX):
        ref = t_all.at[x]
        send(ref, ref, t_ss.at[s], t_rs.at[s], at(x_=(x + s) % NX))

    ri, ci = rows_of((128, 128)), lanes_of((128, 128))
    perm = ((ri // 8 == ci % 16) & (ri % 8 == (ci % 32) // 16 * 4 + ci // 32)).astype(BF16)

    def b_second(c):
        for s in range(1, NZ):
            wait_recv(b1_recv.at[c, (z - s + NZ) % NZ], b1_ss.at[c, s], b1_rs.at[c, s])
        blocks = [b1_recv[c, zz].astype(F32) for zz in range(NZ)]
        for hd in range(NH):
            rows = [blk[hd * 24 : hd * 24 + 24] for blk in blocks] + [jnp.zeros((64, 128), F32)]
            stack = jnp.concatenate(rows, axis=0).astype(BF16)
            bt = lax.dot_general(perm, stack, (((1,), (1,)), ((), ())), preferred_element_type=F32)
            rest = bt[:, 128:]
            fold = jnp.where(low, rest[:64], pltpu.roll(rest[64:], 64, 1))
            b2_send[c, hd, 0:128] = bt[:, :128].astype(BF16)
            b2_send[c, hd, 128:192] = fold.astype(BF16)
        for n, (e, f) in enumerate(y_offsets):
            hd = (h + e) % NH
            target = at(h_=hd, l_=(l + f) % NL)
            send(b2_send.at[c, hd], b_all.at[c, h, col], b2_ss.at[c, n], b2_rs.at[c, n], target)
        send(b2_send.at[c, h], b_all.at[c, h, col], fw_ss.at[c, 7], fw_rs.at[c, 7], sibling)
        b_all[c, h, col] = b2_send[c, h]

    def b_block(c, n, k_):
        e, f = y_offsets[n] if n < 7 else (0, 0)
        return b_all.at[c, (h + e) % NH, col_id((l - f + NL) % NL, k_)]

    def b_forward(c):
        for n in range(7):
            ref = b_block(c, n, k)
            wait_recv(ref, b2_ss.at[c, n], b2_rs.at[c, n])
            send(ref, ref, fw_ss.at[c, n], fw_rs.at[c, n], sibling)

    def b_forwarded(c):
        for n in range(8):
            wait_recv(b_block(c, n, 1 - k), fw_ss.at[c, n], fw_rs.at[c, n])

    b_second(0)
    b_second(1)
    wait_recv(a_blk.at[z, 1 - h], am_ss.at[0], am_rs.at[0])
    a_first(1)
    a_second()
    b_forward(0)
    for part in range(2):
        for kind in (1, -1, 3, -3, 4) if part == 0 else kinds:
            a_wait(part, kind)
    for zp in range(4):
        for hh in range(2):
            b0, b1 = a_blk[2 * zp, hh].astype(F32), a_blk[2 * zp + 1, hh].astype(F32)
            for ah in range(2):
                both = jnp.concatenate([b0[ah * 24 : ah * 24 + 24], b1[ah * 24 : ah * 24 + 24]], axis=0)
                both = both.astype(BF16)
                cols = slice(ah * 512, (ah + 1) * 512)
                r = zp * 48
                split = min(max(128 - r, 0), 48)
                if split > 0:
                    a_all[hh * 128 + r : hh * 128 + r + split, cols] = both[:split]
                if split < 48:
                    start = 256 + hh * 64 + r + split - 128
                    a_all[start : start + 48 - split, cols] = both[split:]

    def unit(c, u):
        rows = []
        for g in range(2):
            lg = 2 * u + g
            for kk in range(NK):
                m = col_id(lg, kk)
                m0, m1 = b_all[c, 0, m, 0:128], b_all[c, 1, m, 0:128]
                f0, f1 = b_all[c, 0, m, 128:192].astype(F32), b_all[c, 1, m, 128:192].astype(F32)
                top = jnp.where(low, f0, pltpu.roll(f1, 64, 1))
                bottom = jnp.where(low, pltpu.roll(f0, 64, 1), f1)
                rest = jnp.concatenate([top, bottom], axis=0).astype(BF16)
                rows.append(jnp.concatenate([m0, m1, rest], axis=1))
        lhs = jnp.concatenate(rows, axis=0)
        for jj in range(4):
            whole = jnp.dot(lhs, a_all[:, jj * 256 : (jj + 1) * 256], preferred_element_type=F32)
            for j in (2 * jj, 2 * jj + 1):
                for g in range(2):
                    prod = whole[g * 256 : (g + 1) * 256, (j % 2) * 128 : (j % 2) * 128 + 128]
                    prod = prod.reshape(2, 16, 8, 128)
                    row = g * 256 + (j % 2) * 128 + (j // 2) * 32
                    for i in range(8):
                        q0 = prod[:, 2 * i].reshape(16, 128).astype(BF16)
                        q1 = prod[:, 2 * i + 1].reshape(16, 128).astype(BF16)
                        e = jnp.where(low16, q0, pltpu.roll(q1, 64, 1))
                        o = jnp.where(low16, pltpu.roll(q0, 64, 1), q1)
                        integral[row : row + 16, i * 128 : (i + 1) * 128] = e
                        integral[row + 16 : row + 32, i * 128 : (i + 1) * 128] = o
        total = jnp.dot(integral[:, 0:512], t_all[2 * c], preferred_element_type=F32)
        total += jnp.dot(integral[:, 512:1024], t_all[2 * c + 1], preferred_element_type=F32)
        for g in range(2):
            for t in range(2):
                part = total[g * 256 : (g + 1) * 256, t * 128 : (t + 1) * 128]
                acc[2 * u + g, t] = part if c == 0 else acc[2 * u + g, t] + part

    for s in range(1, NX):
        wait_recv(t_all.at[(x - s + NX) % NX], t_ss.at[s], t_rs.at[s])
    b_forwarded(0)
    unit(0, 0)
    b_forward(1)
    unit(0, 1)
    b_forwarded(1)

    def mine(u, half, x_):
        return jnp.concatenate([strided(acc.at[2 * u + g], half * 128 + x_, 32, 4) for g in range(2)], axis=0)

    def core_send(u):
        for x_ in range(NX):
            c_send[u, x_] = mine(u, 1 - k, x_).astype(BF16)
        send(c_send.at[u], c_recv.at[u], c_ss.at[u], c_rs.at[u], sibling)

    def x_exchange(u):
        wait_recv(c_recv.at[u], c_ss.at[u], c_rs.at[u])
        for n in range(1, NX):
            x_ = (x + n) % NX
            x_send[u, n] = (mine(u, k, x_) + c_recv[u, x_].astype(F32)).astype(BF16)
            send(x_send.at[u, n], x_recv.at[u, n], x_ss.at[u, n], x_rs.at[u, n], at(x_=x_))

    def x_sum(u):
        own = mine(u, k, x) + c_recv[u, x].astype(F32)
        for n in range(1, NX):
            wait_recv(x_recv.at[u, n], x_ss.at[u, n], x_rs.at[u, n])
            own += x_recv[u, n].astype(F32)
        for g in range(2):
            put(s_v.at[2 * u + g], own[g * 32 : g * 32 + 32])

    unit(1, 0)
    core_send(0)
    unit(1, 1)
    core_send(1)
    flush()
    x_exchange(0)
    x_exchange(1)
    x_sum(0)
    x_sum(1)

    def rows_for(z_):
        both = [strided(s_v.at[2 * half + z_ // 4], z_ % 4, 8, 4) for half in range(NH)]
        return jnp.concatenate(both, axis=0)

    for n in range(1, NZ):
        z_ = (z + n) % NZ
        z_send[n] = rows_for(z_).astype(BF16)
        send(z_send.at[n], z_recv.at[n], z_ss.at[n], z_rs.at[n], at(z_=z_))
    own = rows_for(z)
    flush()
    for n in range(1, NZ):
        wait_recv(z_recv.at[n], z_ss.at[n], z_rs.at[n])
        own += z_recv[n].astype(F32)
    for n in range(8):
        s2_v[n] = own[2 * n : 2 * n + 2]
    for n, (e, f) in enumerate(y_offsets):
        h_, l_ = (h + e) % NH, (l + f) % NL
        send(s2_v.at[h_ * NL + l_], y_recv.at[n], y_ss.at[n], y_rs.at[n], at(h_=h_, l_=l_))
    lane256 = lanes_of((1, 256))
    energy = jnp.zeros((1, 256), F32)
    for n in range(16):
        energy += jnp.where(lane256 // 16 == n, oo[n], 0.0) + jnp.where(lane256 % 16 == n, oo[n], 0.0)
    own = s2_v[h * NL + l]
    for n in range(len(y_offsets)):
        wait_recv(y_recv.at[n], y_ss.at[n], y_rs.at[n])
        own += y_recv[n]
    for j in range(2):
        out[j] = own[j : j + 1] / (oa[j] + ob[0] - energy)

    flush()


def body(fa, fb, fo, sa, sb, tau, oa, ob, oo):
    vmem = pl.BlockSpec(memory_space=pltpu.VMEM)
    smem = pl.BlockSpec(memory_space=pltpu.SMEM)
    hbm = pl.BlockSpec(memory_space=pl.ANY)
    dma = pltpu.SemaphoreType.DMA
    scratch = [
        pltpu.VMEM((384, 512), F32),
        pltpu.VMEM((4, 192, 128), F32),
        pltpu.VMEM((2, 384, 128), F32),
        pltpu.VMEM((512, 256), BF16),
        pltpu.VMEM((2, 512, 128), F32),
        pltpu.VMEM((2, 8, 48, 128), BF16),
        pltpu.VMEM((2, 8, 48, 128), BF16),
        pltpu.VMEM((2, 2, 192, 128), BF16),
        pltpu.VMEM((2, 2, 8, 192, 128), BF16),
        pltpu.VMEM((8, 2, 48, 512), BF16),
        pltpu.VMEM((48, 512), BF16),
        pltpu.VMEM((384, 1024), BF16),
        pltpu.VMEM((4, 512, 256), BF16),
        pltpu.VMEM((512, 1024), BF16),
        pltpu.VMEM((4, 2, 256, 128), F32),
        pltpu.VMEM((2, 4, 64, 256), BF16),
        pltpu.VMEM((2, 4, 64, 256), BF16),
        pltpu.VMEM((2, 4, 64, 256), BF16),
        pltpu.VMEM((2, 4, 64, 256), BF16),
        pltpu.VMEM((4, 2, 32, 128), F32),
        pltpu.VMEM((8, 16, 256), BF16),
        pltpu.VMEM((8, 16, 256), BF16),
        pltpu.VMEM((8, 2, 256), F32),
        pltpu.VMEM((8, 2, 256), F32),
        dma((8,)),
        dma((2, 8)), dma((2, 8)),
        dma((2, 8)), dma((2, 8)),
        dma((2, 8)), dma((2, 8)),
        dma((1,)), dma((1,)),
        dma((2, 7)), dma((2, 7)),
        dma((4,)), dma((4,)),
        dma((2,)), dma((2,)),
        dma((2, 4)), dma((2, 4)),
        dma((8,)), dma((8,)),
        dma((8,)), dma((8,)),
    ]
    return pl.pallas_call(
        kernel,
        out_shape=jax.ShapeDtypeStruct((2, 1, 256), F32),
        in_specs=[hbm, hbm, hbm, vmem, vmem, hbm, smem, smem, smem],
        out_specs=vmem,
        scratch_shapes=scratch,
        compiler_params=pltpu.CompilerParams(
            collective_id=0, has_side_effects=True, vmem_limit_bytes=60 * 1024 * 1024
        ),
        name="ladder",
    )(
        fa.reshape(384, 512),
        fb.reshape(192, 512),
        fo.reshape(384, 512),
        sa,
        sb.T,
        tau.reshape(512, 256),
        oa,
        ob,
        oo,
    )


def solution(mesh):
    return jax.shard_map(
        body,
        mesh=mesh,
        in_specs=(
            P("dev", None, None),
            P("dev", "col", None),
            P("dev", None, None),
            P(),
            P(None, "col"),
            P("col", "dev", None),
            P("col"),
            P("dev"),
            P(),
        ),
        out_specs=P("col", "dev", None),
        check_vma=False,
    )
```

```python
import jax
import jax.numpy as jnp
from jax import lax
from jax.experimental import pallas as pl
from jax.experimental.pallas import tpu as pltpu
from jax.sharding import PartitionSpec as P

MESH = pl.DeviceIdType.MESH
F32 = jnp.float32
BF16 = jnp.bfloat16
HIGHEST = lax.Precision.HIGHEST
NH, NZ, NX, NL, NK = 2, 8, 4, 4, 2


def lanes_of(shape):
    return lax.broadcasted_iota(jnp.int32, shape, len(shape) - 1)


def rows_of(shape):
    return lax.broadcasted_iota(jnp.int32, shape, 0)


def spread(singles, rows):
    pick = (rows_of((rows * 8, rows)) // 8 == lanes_of((rows * 8, rows))).astype(F32)
    across = (rows_of((16, 128)) == lanes_of((16, 128)) % 16).astype(F32)
    first = lax.dot_general(pick, singles, (((1,), (0,)), ((), ())), precision=HIGHEST)
    full = jnp.dot(first, across, precision=HIGHEST)
    same = rows_of((rows * 8, 128)) % 8 == lanes_of((rows * 8, 128)) // 16
    return jnp.where(same, full, 0.0)


def strided(ref, start, size, stride):
    tiles = [ref[t, pl.ds(start, size, stride=stride), :] for t in range(ref.shape[0])]
    return jnp.concatenate(tiles, axis=1)


def put(ref, value):
    for t in range(ref.shape[0]):
        ref[t] = value[:, t * 128 : (t + 1) * 128]


def kernel(
    fa, fb, fo, sa, sb, tau, oa, ob, oo, out,
    fo_v, fb_v, fa_v, tau_v, tf_v,
    b1_send, b1_recv, b2_send, b_all,
    a_blk, a_mir, a_all, t_all, integral, acc,
    c_send, c_recv, x_send, x_recv, s_v, z_send, z_recv, s2_v, y_recv,
    load_sem, b1_ss, b1_rs, b2_ss, b2_rs, rl_ss, rl_rs, fw_ss, fw_rs, am_ss, am_rs, a_ss, a_rs,
    t_ss, t_rs, c_ss, c_rs, x_ss, x_rs, z_ss, z_rs, y_ss, y_rs,
):
    col = lax.axis_index("col")
    dev = lax.axis_index("dev")
    l, k = col // NK, col % NK
    h, z, x = dev // (NZ * NX), (dev // NX) % NZ, dev % NX
    sent = []

    def col_id(l_, k_):
        return l_ * NK + k_

    def at(h_=h, z_=z, x_=x, l_=l, k_=k):
        return (col_id(l_, k_), (h_ * NZ + z_) * NX + x_)

    def remote(src, dst, ss, rs, target):
        return pltpu.make_async_remote_copy(
            src_ref=src, dst_ref=dst, send_sem=ss, recv_sem=rs, device_id=target, device_id_type=MESH
        )

    def send(src, dst, ss, rs, target):
        copy = remote(src, dst, ss, rs, target)
        copy.start()
        sent.append(copy)

    def flush():
        while sent:
            sent.pop().wait_send()

    sibling = at(k_=1 - k)

    def wait_recv(dst, ss, rs):
        remote(dst, dst, ss, rs, sibling).wait_recv()

    ml = NL - 1 - l
    own_lanes = pl.ds(pl.multiple_of(l * 128, 128), 128)
    mir_lanes = pl.ds(pl.multiple_of(ml * 128, 128), 128)
    loads = [
        pltpu.make_async_copy(fo, fo_v, load_sem.at[0]),
        pltpu.make_async_copy(fa.at[:, mir_lanes], fa_v.at[0], load_sem.at[5]),
        pltpu.make_async_copy(fa.at[:, own_lanes], fa_v.at[1], load_sem.at[6]),
        pltpu.make_async_copy(tau, tau_v, load_sem.at[7]),
    ]
    loads[1:1] = [
        pltpu.make_async_copy(fb.at[:, t * 128 : (t + 1) * 128], fb_v.at[t], load_sem.at[1 + t])
        for t in range(4)
    ]
    for load in loads[:5]:
        load.start()

    y_offsets = [(e, f) for e in range(NH) for f in range(NL) if (e, f) != (0, 0)]
    everyone = [at(z_=(z + s) % NZ) for s in range(1, NZ)]
    everyone += [at(x_=(x + s) % NX) for s in range(1, NX)]
    everyone += [at(h_=(h + e) % NH, l_=(l + f) % NL) for e, f in y_offsets]
    everyone += [sibling]
    barrier = pltpu.get_barrier_semaphore()
    for peer in everyone:
        pl.semaphore_signal(barrier, inc=1, device_id=peer, device_id_type=MESH)

    for load in loads[5:]:
        load.start()

    lane128 = lanes_of((1, 128))
    low = lane128 < 64
    low16 = lanes_of((16, 128)) < 64

    pb = spread(sb[...], 8)
    for load in loads[:5]:
        load.wait()
    parts = [[] for _ in range(8)]
    for g in range(3):
        prod = jnp.dot(pb, fo_v[g * 128 : (g + 1) * 128, :], precision=HIGHEST)
        for b in range(8):
            parts[b].append(strided(fb_v, g * 64 + b, 8, 8) - prod[b * 8 : (b + 1) * 8])
    stacked = []
    for b in range(8):
        whole = jnp.concatenate(parts[b], axis=0)
        stacked.append(jnp.concatenate([whole[:, t * 128 : (t + 1) * 128] for t in range(4)], axis=0))
    quarter = lane128 % 64 < 32
    eighth = lane128 % 32 < 16
    ys = []
    for bq in range(2):
        x0, x1, x2, x3 = stacked[bq * 4 : bq * 4 + 4]
        u0 = jnp.where(low, x0, pltpu.roll(x2, 64, 1))
        u2 = jnp.where(low, pltpu.roll(x0, 64, 1), x2)
        u1 = jnp.where(low, x1, pltpu.roll(x3, 64, 1))
        u3 = jnp.where(low, pltpu.roll(x1, 64, 1), x3)
        ys.append([
            jnp.where(quarter, u0, pltpu.roll(u1, 32, 1)),
            jnp.where(quarter, pltpu.roll(u0, 96, 1), u1),
            jnp.where(quarter, u2, pltpu.roll(u3, 32, 1)),
            jnp.where(quarter, pltpu.roll(u2, 96, 1), u3),
        ])
    for j in range(4):
        y0, y1 = ys[0][j], ys[1][j]
        halves = (
            jnp.where(eighth, y0, pltpu.roll(y1, 16, 1)),
            jnp.where(eighth, pltpu.roll(y0, 112, 1), y1),
        )
        for c in range(2):
            for tt in range(2):
                y = halves[c]
                piece = jnp.concatenate(
                    [y[tt * 24 : tt * 24 + 24], y[(2 + tt) * 24 : (2 + tt) * 24 + 24]], axis=0
                )
                b1_send[c, tt * 4 + j] = piece.astype(BF16)

    pl.semaphore_wait(barrier, len(everyone))

    for c in range(2):
        for s in range(1, NZ):
            zt = (z + s) % NZ
            send(b1_send.at[c, zt], b1_recv.at[c, z], b1_ss.at[c, s], b1_rs.at[c, s], at(z_=zt))
        b1_recv[c, z] = b1_send[c, z]

    pa = spread(sa[...].T, 16)

    def dress_a(which):
        half = [[], []]
        for g in range(3):
            lanes = mir_lanes if which == 0 else own_lanes
            prod = jnp.dot(pa, fo_v[g * 128 : (g + 1) * 128, lanes], precision=HIGHEST)
            rows = []
            for a in range(16):
                d = fa_v[which, pl.ds(g * 128 + a, 8, stride=16), :] - prod[a * 8 : (a + 1) * 8]
                rows.append(d)
            for ah in range(2):
                lane_tiles = []
                for pair in range(4):
                    d0, d1 = rows[ah * 8 + pair * 2], rows[ah * 8 + pair * 2 + 1]
                    r0, r1 = pltpu.roll(d0, 64, 1), pltpu.roll(d1, 64, 1)
                    e0 = jnp.where(k == 0, d0, r0)
                    e1 = jnp.where(k == 0, r1, d1)
                    lane_tiles.append(jnp.where(low, e0, e1))
                half[ah].append(jnp.concatenate(lane_tiles, axis=1))
        return jnp.concatenate(half[0] + half[1], axis=0).astype(BF16)

    kinds = [1, -1, 2, -2, 3, -3, 4]

    def a_send(source, part, kind, by):
        ref = a_blk.at[source % NZ, h if part == 0 else 1 - h]
        n = kinds.index(kind)
        send(ref, ref, a_ss.at[part, n], a_rs.at[part, n], at(z_=(z + by + NZ) % NZ))

    def a_wait(part, kind):
        ref = a_blk.at[(z - kind + NZ) % NZ, h if part == 0 else 1 - h]
        n = kinds.index(kind)
        wait_recv(ref, a_ss.at[part, n], a_rs.at[part, n])

    def a_first(part):
        for kind in (2, -2, 1, -1):
            a_send(z, part, kind, kind)

    def a_second(part):
        a_wait(part, 2)
        a_send(z - 2 + NZ, part, 3, 1)
        if part == 0:
            a_send(z - 2 + NZ, part, 4, 2)
        a_wait(part, -2)
        a_send(z + 2, part, -3, -1)
        if part == 1:
            a_send(z + 2, part, 4, -2)

    loads[5].wait()
    a_mir[...] = dress_a(0)
    send(a_mir, a_blk.at[z, h], am_ss.at[0], am_rs.at[0], at(h_=1 - h, l_=ml))
    loads[6].wait()
    a_blk[z, h] = dress_a(1)
    a_first(0)

    loads[7].wait()
    put(tf_v, tau_v[...].astype(F32))
    for d in range(8):
        for e in range(2):
            t_all[x, d * 64 + e * 32 : d * 64 + e * 32 + 32, :] = strided(
                tf_v, e * 256 + d, 32, 8
            ).astype(BF16)
    for s in range(1, NX):
        ref = t_all.at[x]
        send(ref, ref, t_ss.at[s], t_rs.at[s], at(x_=(x + s) % NX))

    ri, ci = rows_of((128, 128)), lanes_of((128, 128))
    perm = ((ri // 8 == ci % 16) & (ri % 8 == (ci % 32) // 16 * 4 + ci // 32)).astype(BF16)

    def b_second(c):
        for s in range(1, NZ):
            wait_recv(b1_recv.at[c, (z - s + NZ) % NZ], b1_ss.at[c, s], b1_rs.at[c, s])
        blocks = [b1_recv[c, zz].astype(F32) for zz in range(NZ)]
        for hd in range(NH):
            rows = [blk[hd * 24 : hd * 24 + 24] for blk in blocks] + [jnp.zeros((64, 128), F32)]
            stack = jnp.concatenate(rows, axis=0).astype(BF16)
            bt = lax.dot_general(perm, stack, (((1,), (1,)), ((), ())), preferred_element_type=F32)
            rest = bt[:, 128:]
            fold = jnp.where(low, rest[:64], pltpu.roll(rest[64:], 64, 1))
            b2_send[c, hd, 0:128] = bt[:, :128].astype(BF16)
            b2_send[c, hd, 128:192] = fold.astype(BF16)
        for n, (hd, ld) in enumerate([(h, 2 - p), (h, partner), (1 - h, i0), (1 - h, 3 - i3)]):
            slot = (n // 2) * NL + l
            target = at(h_=hd, l_=ld)
            send(b2_send.at[c, hd], b_all.at[c, h, col], b2_ss.at[c, n], b2_rs.at[c, slot], target)
        send(b2_send.at[c, h], b_all.at[c, h, col], fw_ss.at[c, 0], fw_rs.at[c, l], sibling)
        b_all[c, h, col] = b2_send[c, h]

    p = l // 2
    partner = l + 1 - 2 * (l % 2)
    i0, i3 = (NL - 1 - l) // 3, l // 3

    def direct(l_):
        outer = ((l_ + 1) // 2 + 1) % 2
        right = l_ // 2
        named = []
        for n in range(3):
            left = outer * (3 - n) + (1 - outer) * (2, 3, 0)[n]
            half = outer + (1 - outer) * (0, 0, 1)[n]
            named.append((half, left * (1 - right) + (3 - left) * right))
        return named

    def b_block(c, name, k_):
        return b_all.at[c, (h + name[0]) % NH, col_id(name[1], k_)]

    def b_forward(c, name, n):
        ref = b_block(c, name, k)
        send(ref, ref, fw_ss.at[c, n], fw_rs.at[c, name[0] * NL + name[1]], sibling)

    def b_direct(c):
        for n, name in enumerate([(0, partner)] + direct(l)):
            ref = b_block(c, name, k)
            slot = name[0] * NL + name[1]
            wait_recv(ref, b2_ss.at[c, 0], b2_rs.at[c, slot])
            if n > 0:
                send(ref, ref, rl_ss.at[c, n], rl_rs.at[c, slot], at(l_=partner))
            b_forward(c, name, 1 + n)

    def b_relayed(c):
        for n, name in enumerate(direct(partner)):
            slot = name[0] * NL + name[1]
            wait_recv(b_block(c, name, k), rl_ss.at[c, 0], rl_rs.at[c, slot])
            b_forward(c, name, 5 + n)

    def b_forwarded(c, u):
        for half in range(NH):
            for l_ in (2 * u, 2 * u + 1):
                wait_recv(b_block(c, (half, l_), 1 - k), fw_ss.at[c, 0], fw_rs.at[c, half * NL + l_])

    b_second(0)
    b_second(1)
    wait_recv(a_blk.at[z, 1 - h], am_ss.at[0], am_rs.at[0])
    a_first(1)
    b_direct(0)
    a_second(0)
    b_relayed(0)
    a_second(1)
    b_direct(1)
    for part in range(2):
        for kind in (1, -1, 3, -3, 4):
            a_wait(part, kind)
    for zp in range(4):
        for hh in range(2):
            b0, b1 = a_blk[2 * zp, hh].astype(F32), a_blk[2 * zp + 1, hh].astype(F32)
            for ah in range(2):
                both = jnp.concatenate([b0[ah * 24 : ah * 24 + 24], b1[ah * 24 : ah * 24 + 24]], axis=0)
                both = both.astype(BF16)
                cols = slice(ah * 512, (ah + 1) * 512)
                r = zp * 48
                split = min(max(128 - r, 0), 48)
                if split > 0:
                    a_all[hh * 128 + r : hh * 128 + r + split, cols] = both[:split]
                if split < 48:
                    start = 256 + hh * 64 + r + split - 128
                    a_all[start : start + 48 - split, cols] = both[split:]

    def unit(c, u):
        rows = []
        for g in range(2):
            lg = 2 * u + g
            for kk in range(NK):
                m = col_id(lg, kk)
                m0, m1 = b_all[c, 0, m, 0:128], b_all[c, 1, m, 0:128]
                f0, f1 = b_all[c, 0, m, 128:192].astype(F32), b_all[c, 1, m, 128:192].astype(F32)
                top = jnp.where(low, f0, pltpu.roll(f1, 64, 1))
                bottom = jnp.where(low, pltpu.roll(f0, 64, 1), f1)
                rest = jnp.concatenate([top, bottom], axis=0).astype(BF16)
                rows.append(jnp.concatenate([m0, m1, rest], axis=1))
        lhs = jnp.concatenate(rows, axis=0)
        for jj in range(4):
            whole = jnp.dot(lhs, a_all[:, jj * 256 : (jj + 1) * 256], preferred_element_type=F32)
            for j in (2 * jj, 2 * jj + 1):
                for g in range(2):
                    prod = whole[g * 256 : (g + 1) * 256, (j % 2) * 128 : (j % 2) * 128 + 128]
                    prod = prod.reshape(2, 16, 8, 128)
                    row = g * 256 + (j % 2) * 128 + (j // 2) * 32
                    for i in range(8):
                        q0 = prod[:, 2 * i].reshape(16, 128).astype(BF16)
                        q1 = prod[:, 2 * i + 1].reshape(16, 128).astype(BF16)
                        e = jnp.where(low16, q0, pltpu.roll(q1, 64, 1))
                        o = jnp.where(low16, pltpu.roll(q0, 64, 1), q1)
                        integral[row : row + 16, i * 128 : (i + 1) * 128] = e
                        integral[row + 16 : row + 32, i * 128 : (i + 1) * 128] = o
        total = jnp.dot(integral[:, 0:512], t_all[2 * c], preferred_element_type=F32)
        total += jnp.dot(integral[:, 512:1024], t_all[2 * c + 1], preferred_element_type=F32)
        for g in range(2):
            for t in range(2):
                part = total[g * 256 : (g + 1) * 256, t * 128 : (t + 1) * 128]
                acc[2 * u + g, t] = part if c == 0 else acc[2 * u + g, t] + part

    for s in range(1, NX):
        wait_recv(t_all.at[(x - s + NX) % NX], t_ss.at[s], t_rs.at[s])
    b_forwarded(0, 0)
    unit(0, 0)
    b_forwarded(0, 1)
    b_relayed(1)
    unit(0, 1)
    b_forwarded(1, 0)

    def mine(u, half, x_):
        return jnp.concatenate([strided(acc.at[2 * u + g], half * 128 + x_, 32, 4) for g in range(2)], axis=0)

    def core_send(u):
        for x_ in range(NX):
            c_send[u, x_] = mine(u, 1 - k, x_).astype(BF16)
        send(c_send.at[u], c_recv.at[u], c_ss.at[u], c_rs.at[u], sibling)

    def x_exchange(u):
        wait_recv(c_recv.at[u], c_ss.at[u], c_rs.at[u])
        for n in range(1, NX):
            x_ = (x + n) % NX
            x_send[u, n] = (mine(u, k, x_) + c_recv[u, x_].astype(F32)).astype(BF16)
            send(x_send.at[u, n], x_recv.at[u, n], x_ss.at[u, n], x_rs.at[u, n], at(x_=x_))

    def x_sum(u):
        own = mine(u, k, x) + c_recv[u, x].astype(F32)
        for n in range(1, NX):
            wait_recv(x_recv.at[u, n], x_ss.at[u, n], x_rs.at[u, n])
            own += x_recv[u, n].astype(F32)
        for g in range(2):
            put(s_v.at[2 * u + g], own[g * 32 : g * 32 + 32])

    unit(1, 0)
    core_send(0)
    b_forwarded(1, 1)
    unit(1, 1)
    core_send(1)
    x_exchange(0)
    x_exchange(1)
    flush()
    x_sum(0)
    x_sum(1)

    def rows_for(z_):
        both = [strided(s_v.at[2 * half + z_ // 4], z_ % 4, 8, 4) for half in range(NH)]
        return jnp.concatenate(both, axis=0)

    for n in range(1, NZ):
        z_ = (z + n) % NZ
        z_send[n] = rows_for(z_).astype(BF16)
        send(z_send.at[n], z_recv.at[n], z_ss.at[n], z_rs.at[n], at(z_=z_))
    own = rows_for(z)
    flush()
    for n in range(1, NZ):
        wait_recv(z_recv.at[n], z_ss.at[n], z_rs.at[n])
        own += z_recv[n].astype(F32)
    for n in range(8):
        s2_v[n] = own[2 * n : 2 * n + 2]
    for n, (e, f) in enumerate(y_offsets):
        h_, l_ = (h + e) % NH, (l + f) % NL
        send(s2_v.at[h_ * NL + l_], y_recv.at[n], y_ss.at[n], y_rs.at[n], at(h_=h_, l_=l_))
    lane256 = lanes_of((1, 256))
    energy = jnp.zeros((1, 256), F32)
    for n in range(16):
        energy += jnp.where(lane256 // 16 == n, oo[n], 0.0) + jnp.where(lane256 % 16 == n, oo[n], 0.0)
    own = s2_v[h * NL + l]
    for n in range(len(y_offsets)):
        wait_recv(y_recv.at[n], y_ss.at[n], y_rs.at[n])
        own += y_recv[n]
    for j in range(2):
        out[j] = own[j : j + 1] / (oa[j] + ob[0] - energy)

    flush()


def body(fa, fb, fo, sa, sb, tau, oa, ob, oo):
    vmem = pl.BlockSpec(memory_space=pltpu.VMEM)
    smem = pl.BlockSpec(memory_space=pltpu.SMEM)
    hbm = pl.BlockSpec(memory_space=pl.ANY)
    dma = pltpu.SemaphoreType.DMA
    scratch = [
        pltpu.VMEM((384, 512), F32),
        pltpu.VMEM((4, 192, 128), F32),
        pltpu.VMEM((2, 384, 128), F32),
        pltpu.VMEM((512, 256), BF16),
        pltpu.VMEM((2, 512, 128), F32),
        pltpu.VMEM((2, 8, 48, 128), BF16),
        pltpu.VMEM((2, 8, 48, 128), BF16),
        pltpu.VMEM((2, 2, 192, 128), BF16),
        pltpu.VMEM((2, 2, 8, 192, 128), BF16),
        pltpu.VMEM((8, 2, 48, 512), BF16),
        pltpu.VMEM((48, 512), BF16),
        pltpu.VMEM((384, 1024), BF16),
        pltpu.VMEM((4, 512, 256), BF16),
        pltpu.VMEM((512, 1024), BF16),
        pltpu.VMEM((4, 2, 256, 128), F32),
        pltpu.VMEM((2, 4, 64, 256), BF16),
        pltpu.VMEM((2, 4, 64, 256), BF16),
        pltpu.VMEM((2, 4, 64, 256), BF16),
        pltpu.VMEM((2, 4, 64, 256), BF16),
        pltpu.VMEM((4, 2, 32, 128), F32),
        pltpu.VMEM((8, 16, 256), BF16),
        pltpu.VMEM((8, 16, 256), BF16),
        pltpu.VMEM((8, 2, 256), F32),
        pltpu.VMEM((8, 2, 256), F32),
        dma((8,)),
        dma((2, 8)), dma((2, 8)),
        dma((2, 8)), dma((2, 8)),
        dma((2, 8)), dma((2, 8)),
        dma((2, 8)), dma((2, 8)),
        dma((1,)), dma((1,)),
        dma((2, 7)), dma((2, 7)),
        dma((4,)), dma((4,)),
        dma((2,)), dma((2,)),
        dma((2, 4)), dma((2, 4)),
        dma((8,)), dma((8,)),
        dma((8,)), dma((8,)),
    ]
    return pl.pallas_call(
        kernel,
        out_shape=jax.ShapeDtypeStruct((2, 1, 256), F32),
        in_specs=[hbm, hbm, hbm, vmem, vmem, hbm, smem, smem, smem],
        out_specs=vmem,
        scratch_shapes=scratch,
        compiler_params=pltpu.CompilerParams(
            collective_id=0, has_side_effects=True, vmem_limit_bytes=60 * 1024 * 1024
        ),
        name="ladder",
    )(
        fa.reshape(384, 512),
        fb.reshape(192, 512),
        fo.reshape(384, 512),
        sa,
        sb.T,
        tau.reshape(512, 256),
        oa,
        ob,
        oo,
    )


def solution(mesh):
    return jax.shard_map(
        body,
        mesh=mesh,
        in_specs=(
            P("dev", None, None),
            P("dev", "col", None),
            P("dev", None, None),
            P(),
            P(None, "col"),
            P("col", "dev", None),
            P("col"),
            P("dev"),
            P(),
        ),
        out_specs=P("col", "dev", None),
        check_vma=False,
    )
```

```python
import jax
import jax.numpy as jnp
from jax import lax
from jax.experimental import pallas as pl
from jax.experimental.pallas import tpu as pltpu
from jax.sharding import PartitionSpec as P

MESH = pl.DeviceIdType.MESH
F32 = jnp.float32
BF16 = jnp.bfloat16
HIGHEST = lax.Precision.HIGHEST
NH, NZ, NX, NL, NK = 2, 8, 4, 4, 2


def lanes_of(shape):
    return lax.broadcasted_iota(jnp.int32, shape, len(shape) - 1)


def rows_of(shape):
    return lax.broadcasted_iota(jnp.int32, shape, 0)


def spread(singles, rows):
    pick = (rows_of((rows * 8, rows)) // 8 == lanes_of((rows * 8, rows))).astype(F32)
    across = (rows_of((16, 128)) == lanes_of((16, 128)) % 16).astype(F32)
    first = lax.dot_general(pick, singles, (((1,), (0,)), ((), ())), precision=HIGHEST)
    full = jnp.dot(first, across, precision=HIGHEST)
    same = rows_of((rows * 8, 128)) % 8 == lanes_of((rows * 8, 128)) // 16
    return jnp.where(same, full, 0.0)


def strided(ref, start, size, stride):
    tiles = [ref[t, pl.ds(start, size, stride=stride), :] for t in range(ref.shape[0])]
    return jnp.concatenate(tiles, axis=1)


def put(ref, value):
    for t in range(ref.shape[0]):
        ref[t] = value[:, t * 128 : (t + 1) * 128]


def kernel(
    fa, fb, fo, sa, sb, tau, oa, ob, oo, out,
    fo_v, fb_v, fa_v, tau_v, tf_v,
    b1_send, b1_recv, b2_send, b_all,
    a_blk, a_mir, a_all, t_all, integral, acc,
    c_send, c_recv, x_send, x_recv, s_v, z_send, z_recv, s2_v, y_recv,
    load_sem, b1_ss, b1_rs, b2_ss, b2_rs, rl_ss, rl_rs, fw_ss, fw_rs, am_ss, am_rs, a_ss, a_rs,
    t_ss, t_rs, c_ss, c_rs, x_ss, x_rs, z_ss, z_rs, y_ss, y_rs,
):
    col = lax.axis_index("col")
    dev = lax.axis_index("dev")
    l, k = col // NK, col % NK
    h, z, x = dev // (NZ * NX), (dev // NX) % NZ, dev % NX
    sent = []

    def col_id(l_, k_):
        return l_ * NK + k_

    def at(h_=h, z_=z, x_=x, l_=l, k_=k):
        return (col_id(l_, k_), (h_ * NZ + z_) * NX + x_)

    def remote(src, dst, ss, rs, target):
        return pltpu.make_async_remote_copy(
            src_ref=src, dst_ref=dst, send_sem=ss, recv_sem=rs, device_id=target, device_id_type=MESH
        )

    def send(src, dst, ss, rs, target):
        copy = remote(src, dst, ss, rs, target)
        copy.start()
        sent.append(copy)

    def flush():
        while sent:
            sent.pop().wait_send()

    sibling = at(k_=1 - k)

    def wait_recv(dst, ss, rs):
        remote(dst, dst, ss, rs, sibling).wait_recv()

    ml = NL - 1 - l
    own_lanes = pl.ds(pl.multiple_of(l * 128, 128), 128)
    mir_lanes = pl.ds(pl.multiple_of(ml * 128, 128), 128)
    loads = [
        pltpu.make_async_copy(fo, fo_v, load_sem.at[0]),
        pltpu.make_async_copy(fa.at[:, mir_lanes], fa_v.at[0], load_sem.at[5]),
        pltpu.make_async_copy(fa.at[:, own_lanes], fa_v.at[1], load_sem.at[6]),
        pltpu.make_async_copy(tau, tau_v, load_sem.at[7]),
    ]
    loads[1:1] = [
        pltpu.make_async_copy(fb.at[:, t * 128 : (t + 1) * 128], fb_v.at[t], load_sem.at[1 + t])
        for t in range(4)
    ]
    for load in loads[:5]:
        load.start()

    y_offsets = [(e, f) for e in range(NH) for f in range(NL) if (e, f) != (0, 0)]
    everyone = [at(z_=(z + s) % NZ) for s in range(1, NZ)]
    everyone += [at(x_=(x + s) % NX) for s in range(1, NX)]
    everyone += [at(h_=(h + e) % NH, l_=(l + f) % NL) for e, f in y_offsets]
    everyone += [sibling]
    barrier = pltpu.get_barrier_semaphore()
    for peer in everyone:
        pl.semaphore_signal(barrier, inc=1, device_id=peer, device_id_type=MESH)

    for load in loads[5:]:
        load.start()

    lane128 = lanes_of((1, 128))
    low = lane128 < 64
    low16 = lanes_of((16, 128)) < 64

    pb = spread(sb[...], 8)
    for load in loads[:5]:
        load.wait()
    parts = [[] for _ in range(8)]
    for g in range(3):
        prod = jnp.dot(pb, fo_v[g * 128 : (g + 1) * 128, :], precision=HIGHEST)
        for b in range(8):
            parts[b].append(strided(fb_v, g * 64 + b, 8, 8) - prod[b * 8 : (b + 1) * 8])
    stacked = []
    for b in range(8):
        whole = jnp.concatenate(parts[b], axis=0)
        stacked.append(jnp.concatenate([whole[:, t * 128 : (t + 1) * 128] for t in range(4)], axis=0))
    quarter = lane128 % 64 < 32
    eighth = lane128 % 32 < 16
    ys = []
    for bq in range(2):
        x0, x1, x2, x3 = stacked[bq * 4 : bq * 4 + 4]
        u0 = jnp.where(low, x0, pltpu.roll(x2, 64, 1))
        u2 = jnp.where(low, pltpu.roll(x0, 64, 1), x2)
        u1 = jnp.where(low, x1, pltpu.roll(x3, 64, 1))
        u3 = jnp.where(low, pltpu.roll(x1, 64, 1), x3)
        ys.append([
            jnp.where(quarter, u0, pltpu.roll(u1, 32, 1)),
            jnp.where(quarter, pltpu.roll(u0, 96, 1), u1),
            jnp.where(quarter, u2, pltpu.roll(u3, 32, 1)),
            jnp.where(quarter, pltpu.roll(u2, 96, 1), u3),
        ])
    for j in range(4):
        y0, y1 = ys[0][j], ys[1][j]
        halves = (
            jnp.where(eighth, y0, pltpu.roll(y1, 16, 1)),
            jnp.where(eighth, pltpu.roll(y0, 112, 1), y1),
        )
        for c in range(2):
            for tt in range(2):
                y = halves[c]
                piece = jnp.concatenate(
                    [y[tt * 24 : tt * 24 + 24], y[(2 + tt) * 24 : (2 + tt) * 24 + 24]], axis=0
                )
                b1_send[c, tt * 4 + j] = piece.astype(BF16)

    pl.semaphore_wait(barrier, len(everyone))

    for c in range(2):
        for s in range(1, NZ):
            zt = (z + s) % NZ
            send(b1_send.at[c, zt], b1_recv.at[c, z], b1_ss.at[c, s], b1_rs.at[c, s], at(z_=zt))
        b1_recv[c, z] = b1_send[c, z]

    pa = spread(sa[...].T, 16)

    def dress_a(which):
        half = [[], []]
        for g in range(3):
            lanes = mir_lanes if which == 0 else own_lanes
            prod = jnp.dot(pa, fo_v[g * 128 : (g + 1) * 128, lanes], precision=HIGHEST)
            rows = []
            for a in range(16):
                d = fa_v[which, pl.ds(g * 128 + a, 8, stride=16), :] - prod[a * 8 : (a + 1) * 8]
                rows.append(d)
            for ah in range(2):
                lane_tiles = []
                for pair in range(4):
                    d0, d1 = rows[ah * 8 + pair * 2], rows[ah * 8 + pair * 2 + 1]
                    r0, r1 = pltpu.roll(d0, 64, 1), pltpu.roll(d1, 64, 1)
                    e0 = jnp.where(k == 0, d0, r0)
                    e1 = jnp.where(k == 0, r1, d1)
                    lane_tiles.append(jnp.where(low, e0, e1))
                half[ah].append(jnp.concatenate(lane_tiles, axis=1))
        return jnp.concatenate(half[0] + half[1], axis=0).astype(BF16)

    kinds = [1, -1, 2, -2, 3, -3, 4]

    def a_send(source, part, kind, by):
        ref = a_blk.at[source % NZ, h if part == 0 else 1 - h]
        n = kinds.index(kind)
        send(ref, ref, a_ss.at[part, n], a_rs.at[part, n], at(z_=(z + by + NZ) % NZ))

    def a_wait(part, kind):
        ref = a_blk.at[(z - kind + NZ) % NZ, h if part == 0 else 1 - h]
        n = kinds.index(kind)
        wait_recv(ref, a_ss.at[part, n], a_rs.at[part, n])

    def a_first(part):
        for kind in (2, -2, 1, -1):
            a_send(z, part, kind, kind)

    def a_second(part):
        a_wait(part, 2)
        a_send(z - 2 + NZ, part, 3, 1)
        if part == 0:
            a_send(z - 2 + NZ, part, 4, 2)
        a_wait(part, -2)
        a_send(z + 2, part, -3, -1)
        if part == 1:
            a_send(z + 2, part, 4, -2)

    loads[5].wait()
    a_mir[...] = dress_a(0)
    send(a_mir, a_blk.at[z, h], am_ss.at[0], am_rs.at[0], at(h_=1 - h, l_=ml))
    loads[6].wait()
    a_blk[z, h] = dress_a(1)
    a_first(0)

    ri, ci = rows_of((128, 128)), lanes_of((128, 128))
    perm = ((ri // 8 == ci % 16) & (ri % 8 == (ci % 32) // 16 * 4 + ci // 32)).astype(BF16)

    def b_second(c):
        for s in range(1, NZ):
            wait_recv(b1_recv.at[c, (z - s + NZ) % NZ], b1_ss.at[c, s], b1_rs.at[c, s])
        blocks = [b1_recv[c, zz].astype(F32) for zz in range(NZ)]
        for hd in range(NH):
            rows = [blk[hd * 24 : hd * 24 + 24] for blk in blocks] + [jnp.zeros((64, 128), F32)]
            stack = jnp.concatenate(rows, axis=0).astype(BF16)
            bt = lax.dot_general(perm, stack, (((1,), (1,)), ((), ())), preferred_element_type=F32)
            rest = bt[:, 128:]
            fold = jnp.where(low, rest[:64], pltpu.roll(rest[64:], 64, 1))
            b2_send[c, hd, 0:128] = bt[:, :128].astype(BF16)
            b2_send[c, hd, 128:192] = fold.astype(BF16)
        for n, (hd, ld) in enumerate([(h, 2 - p), (h, partner), (1 - h, i0), (1 - h, 3 - i3)]):
            slot = (n // 2) * NL + l
            target = at(h_=hd, l_=ld)
            send(b2_send.at[c, hd], b_all.at[c, h, col], b2_ss.at[c, n], b2_rs.at[c, slot], target)
        send(b2_send.at[c, h], b_all.at[c, h, col], fw_ss.at[c, 0], fw_rs.at[c, l], sibling)
        b_all[c, h, col] = b2_send[c, h]

    p = l // 2
    partner = l + 1 - 2 * (l % 2)
    i0, i3 = (NL - 1 - l) // 3, l // 3

    def direct(l_):
        outer = ((l_ + 1) // 2 + 1) % 2
        right = l_ // 2
        named = []
        for n in range(3):
            left = outer * (3 - n) + (1 - outer) * (2, 3, 0)[n]
            half = outer + (1 - outer) * (0, 0, 1)[n]
            named.append((half, left * (1 - right) + (3 - left) * right))
        return named

    def b_block(c, name, k_):
        return b_all.at[c, (h + name[0]) % NH, col_id(name[1], k_)]

    def b_forward(c, name, n):
        ref = b_block(c, name, k)
        send(ref, ref, fw_ss.at[c, n], fw_rs.at[c, name[0] * NL + name[1]], sibling)

    def b_direct(c):
        for n, name in enumerate([(0, partner)] + direct(l)):
            ref = b_block(c, name, k)
            slot = name[0] * NL + name[1]
            wait_recv(ref, b2_ss.at[c, 0], b2_rs.at[c, slot])
            if n > 0:
                send(ref, ref, rl_ss.at[c, n], rl_rs.at[c, slot], at(l_=partner))
            b_forward(c, name, 1 + n)

    def b_relayed(c):
        for n, name in enumerate(direct(partner)):
            slot = name[0] * NL + name[1]
            wait_recv(b_block(c, name, k), rl_ss.at[c, 0], rl_rs.at[c, slot])
            b_forward(c, name, 5 + n)

    def b_forwarded(c, u):
        for half in range(NH):
            for l_ in (2 * u, 2 * u + 1):
                wait_recv(b_block(c, (half, l_), 1 - k), fw_ss.at[c, 0], fw_rs.at[c, half * NL + l_])

    b_second(0)
    b_second(1)

    loads[7].wait()
    put(tf_v, tau_v[...].astype(F32))
    for d in range(8):
        for e in range(2):
            t_all[x, d * 64 + e * 32 : d * 64 + e * 32 + 32, :] = strided(
                tf_v, e * 256 + d, 32, 8
            ).astype(BF16)
    for s in range(1, NX):
        ref = t_all.at[x]
        send(ref, ref, t_ss.at[s], t_rs.at[s], at(x_=(x + s) % NX))

    wait_recv(a_blk.at[z, 1 - h], am_ss.at[0], am_rs.at[0])
    a_first(1)
    b_direct(0)
    a_second(0)
    b_relayed(0)
    a_second(1)
    b_direct(1)
    for part in range(2):
        for kind in (1, -1, 3, -3, 4):
            a_wait(part, kind)
    for zp in range(4):
        for hh in range(2):
            b0, b1 = a_blk[2 * zp, hh].astype(F32), a_blk[2 * zp + 1, hh].astype(F32)
            for ah in range(2):
                both = jnp.concatenate([b0[ah * 24 : ah * 24 + 24], b1[ah * 24 : ah * 24 + 24]], axis=0)
                both = both.astype(BF16)
                cols = slice(ah * 512, (ah + 1) * 512)
                r = zp * 48
                split = min(max(128 - r, 0), 48)
                if split > 0:
                    a_all[hh * 128 + r : hh * 128 + r + split, cols] = both[:split]
                if split < 48:
                    start = 256 + hh * 64 + r + split - 128
                    a_all[start : start + 48 - split, cols] = both[split:]

    def unit(c, u):
        rows = []
        for g in range(2):
            lg = 2 * u + g
            for kk in range(NK):
                m = col_id(lg, kk)
                m0, m1 = b_all[c, 0, m, 0:128], b_all[c, 1, m, 0:128]
                f0, f1 = b_all[c, 0, m, 128:192].astype(F32), b_all[c, 1, m, 128:192].astype(F32)
                top = jnp.where(low, f0, pltpu.roll(f1, 64, 1))
                bottom = jnp.where(low, pltpu.roll(f0, 64, 1), f1)
                rest = jnp.concatenate([top, bottom], axis=0).astype(BF16)
                rows.append(jnp.concatenate([m0, m1, rest], axis=1))
        lhs = jnp.concatenate(rows, axis=0)
        for jj in range(4):
            whole = jnp.dot(lhs, a_all[:, jj * 256 : (jj + 1) * 256], preferred_element_type=F32)
            for j in (2 * jj, 2 * jj + 1):
                for g in range(2):
                    prod = whole[g * 256 : (g + 1) * 256, (j % 2) * 128 : (j % 2) * 128 + 128]
                    prod = prod.reshape(2, 16, 8, 128)
                    row = g * 256 + (j % 2) * 128 + (j // 2) * 32
                    for i in range(8):
                        q0 = prod[:, 2 * i].reshape(16, 128).astype(BF16)
                        q1 = prod[:, 2 * i + 1].reshape(16, 128).astype(BF16)
                        e = jnp.where(low16, q0, pltpu.roll(q1, 64, 1))
                        o = jnp.where(low16, pltpu.roll(q0, 64, 1), q1)
                        integral[row : row + 16, i * 128 : (i + 1) * 128] = e
                        integral[row + 16 : row + 32, i * 128 : (i + 1) * 128] = o
        total = jnp.dot(integral[:, 0:512], t_all[2 * c], preferred_element_type=F32)
        total += jnp.dot(integral[:, 512:1024], t_all[2 * c + 1], preferred_element_type=F32)
        for g in range(2):
            for t in range(2):
                part = total[g * 256 : (g + 1) * 256, t * 128 : (t + 1) * 128]
                acc[2 * u + g, t] = part if c == 0 else acc[2 * u + g, t] + part

    for s in range(1, NX):
        wait_recv(t_all.at[(x - s + NX) % NX], t_ss.at[s], t_rs.at[s])
    b_forwarded(0, 0)
    unit(0, 0)
    b_forwarded(0, 1)
    b_relayed(1)
    unit(0, 1)
    b_forwarded(1, 0)

    def mine(u, half, x_):
        return jnp.concatenate([strided(acc.at[2 * u + g], half * 128 + x_, 32, 4) for g in range(2)], axis=0)

    def core_send(u):
        for x_ in range(NX):
            c_send[u, x_] = mine(u, 1 - k, x_).astype(BF16)
        send(c_send.at[u], c_recv.at[u], c_ss.at[u], c_rs.at[u], sibling)

    def x_exchange(u):
        wait_recv(c_recv.at[u], c_ss.at[u], c_rs.at[u])
        for n in range(1, NX):
            x_ = (x + n) % NX
            x_send[u, n] = (mine(u, k, x_) + c_recv[u, x_].astype(F32)).astype(BF16)
            send(x_send.at[u, n], x_recv.at[u, n], x_ss.at[u, n], x_rs.at[u, n], at(x_=x_))

    def x_sum(u):
        own = mine(u, k, x) + c_recv[u, x].astype(F32)
        for n in range(1, NX):
            wait_recv(x_recv.at[u, n], x_ss.at[u, n], x_rs.at[u, n])
            own += x_recv[u, n].astype(F32)
        for g in range(2):
            put(s_v.at[2 * u + g], own[g * 32 : g * 32 + 32])

    unit(1, 0)
    core_send(0)
    b_forwarded(1, 1)
    unit(1, 1)
    core_send(1)
    x_exchange(0)
    x_exchange(1)
    flush()
    x_sum(0)
    x_sum(1)

    def rows_for(z_):
        both = [strided(s_v.at[2 * half + z_ // 4], z_ % 4, 8, 4) for half in range(NH)]
        return jnp.concatenate(both, axis=0)

    for n in range(1, NZ):
        z_ = (z + n) % NZ
        z_send[n] = rows_for(z_).astype(BF16)
        send(z_send.at[n], z_recv.at[n], z_ss.at[n], z_rs.at[n], at(z_=z_))
    own = rows_for(z)
    flush()
    for n in range(1, NZ):
        wait_recv(z_recv.at[n], z_ss.at[n], z_rs.at[n])
        own += z_recv[n].astype(F32)
    for n in range(8):
        s2_v[n] = own[2 * n : 2 * n + 2]
    for n, (e, f) in enumerate(y_offsets):
        h_, l_ = (h + e) % NH, (l + f) % NL
        send(s2_v.at[h_ * NL + l_], y_recv.at[n], y_ss.at[n], y_rs.at[n], at(h_=h_, l_=l_))
    lane256 = lanes_of((1, 256))
    energy = jnp.zeros((1, 256), F32)
    for n in range(16):
        energy += jnp.where(lane256 // 16 == n, oo[n], 0.0) + jnp.where(lane256 % 16 == n, oo[n], 0.0)
    own = s2_v[h * NL + l]
    for n in range(len(y_offsets)):
        wait_recv(y_recv.at[n], y_ss.at[n], y_rs.at[n])
        own += y_recv[n]
    for j in range(2):
        out[j] = own[j : j + 1] / (oa[j] + ob[0] - energy)

    flush()


def body(fa, fb, fo, sa, sb, tau, oa, ob, oo):
    vmem = pl.BlockSpec(memory_space=pltpu.VMEM)
    smem = pl.BlockSpec(memory_space=pltpu.SMEM)
    hbm = pl.BlockSpec(memory_space=pl.ANY)
    dma = pltpu.SemaphoreType.DMA
    scratch = [
        pltpu.VMEM((384, 512), F32),
        pltpu.VMEM((4, 192, 128), F32),
        pltpu.VMEM((2, 384, 128), F32),
        pltpu.VMEM((512, 256), BF16),
        pltpu.VMEM((2, 512, 128), F32),
        pltpu.VMEM((2, 8, 48, 128), BF16),
        pltpu.VMEM((2, 8, 48, 128), BF16),
        pltpu.VMEM((2, 2, 192, 128), BF16),
        pltpu.VMEM((2, 2, 8, 192, 128), BF16),
        pltpu.VMEM((8, 2, 48, 512), BF16),
        pltpu.VMEM((48, 512), BF16),
        pltpu.VMEM((384, 1024), BF16),
        pltpu.VMEM((4, 512, 256), BF16),
        pltpu.VMEM((512, 1024), BF16),
        pltpu.VMEM((4, 2, 256, 128), F32),
        pltpu.VMEM((2, 4, 64, 256), BF16),
        pltpu.VMEM((2, 4, 64, 256), BF16),
        pltpu.VMEM((2, 4, 64, 256), BF16),
        pltpu.VMEM((2, 4, 64, 256), BF16),
        pltpu.VMEM((4, 2, 32, 128), F32),
        pltpu.VMEM((8, 16, 256), BF16),
        pltpu.VMEM((8, 16, 256), BF16),
        pltpu.VMEM((8, 2, 256), F32),
        pltpu.VMEM((8, 2, 256), F32),
        dma((8,)),
        dma((2, 8)), dma((2, 8)),
        dma((2, 8)), dma((2, 8)),
        dma((2, 8)), dma((2, 8)),
        dma((2, 8)), dma((2, 8)),
        dma((1,)), dma((1,)),
        dma((2, 7)), dma((2, 7)),
        dma((4,)), dma((4,)),
        dma((2,)), dma((2,)),
        dma((2, 4)), dma((2, 4)),
        dma((8,)), dma((8,)),
        dma((8,)), dma((8,)),
    ]
    return pl.pallas_call(
        kernel,
        out_shape=jax.ShapeDtypeStruct((2, 1, 256), F32),
        in_specs=[hbm, hbm, hbm, vmem, vmem, hbm, smem, smem, smem],
        out_specs=vmem,
        scratch_shapes=scratch,
        compiler_params=pltpu.CompilerParams(
            collective_id=0, has_side_effects=True, vmem_limit_bytes=60 * 1024 * 1024
        ),
        name="ladder",
    )(
        fa.reshape(384, 512),
        fb.reshape(192, 512),
        fo.reshape(384, 512),
        sa,
        sb.T,
        tau.reshape(512, 256),
        oa,
        ob,
        oo,
    )


def solution(mesh):
    return jax.shard_map(
        body,
        mesh=mesh,
        in_specs=(
            P("dev", None, None),
            P("dev", "col", None),
            P("dev", None, None),
            P(),
            P(None, "col"),
            P("col", "dev", None),
            P("col"),
            P("dev"),
            P(),
        ),
        out_specs=P("col", "dev", None),
        check_vma=False,
    )
```
